512 devices in a mesh: dp: 16 (over y, core), seq: 32 (over z, x).
Axes of the slice: x: 4, y: 8, z: 8, core: 2. Of those that a mesh axis runs over, the one named last changes fastest.
Arguments:
- queries: bfloat16 [16, 4096, 1024], P('dp', 'seq'), may hold values from -80 to 80
- keys_in: bfloat16 [16, 4096, 1024], P('dp', 'seq'), may hold values from -4 to 4
- values_in: bfloat16 [16, 4096, 1024], P('dp', 'seq'), may hold values from -6 to 6
- cotangent: bfloat16 [16, 4096, 1024], P('dp', 'seq'), may hold values from -6 to 6
- level_slope: float32 [8], replicated, may hold values from -0.4 to 0.2
Outputs:
- grad_queries: bfloat16 [16, 4096, 1024], P('dp', 'seq')
- grad_keys: bfloat16 [16, 4096, 1024], P('dp', 'seq')
- grad_values: bfloat16 [16, 4096, 1024], P('dp', 'seq')
- grad_slope: float32 [8], replicated
The draws below stay inside these ranges and needn't reach their ends.
All inputs are finite; a program needn't handle non-finite values.
Results may differ from the reference program's by a relative error of at most 0.007.
Values may be sent and summed in bfloat16 or wider, within the bound.
No kernel may reach another device: no remote copies, remote signals or barrier semaphores. Data moves between devices by JAX's collectives and lax.ppermute only.
A program may use at most 64 MiB of HBM per device.

```python
import math
import jax
import jax.numpy as jnp
from jax import lax

HEADS = 8
LEAF = 16
HD = 1024
LENGTH = 4096
SEQS = 16


def shared_keys(key):
    return jnp.clip(jax.random.normal(key, (SEQS, LENGTH, HD), jnp.float32), -4.0, 4.0)


def draw_keys_in(key, part):
    base = shared_keys(key)
    return base.astype(jnp.bfloat16)


def draw_queries(key, part):
    key = jax.random.fold_in(key, 7)
    drawn = jnp.clip(jax.random.normal(key, (SEQS, LENGTH, HD), jnp.float32), -4.0, 4.0)
    return drawn.astype(jnp.bfloat16)


def block_scale(key, dims, cuts, low, largest):
    def one(axis_at, parts):
        draws = jax.random.uniform(jax.random.fold_in(jax.random.fold_in(key, 6), axis_at), (parts,), jnp.float32, low / len(cuts), largest / len(cuts))
        return jnp.repeat(jnp.exp(draws), dims[axis_at] // parts).reshape((-1,) + (1,) * (len(dims) - axis_at - 1))

    loudness = one(*cuts[0])
    for cut in cuts[1:]:
        loudness = loudness * one(*cut)
    return loudness


def centred(stream_key, extent, scale, reach, shards=(), dtype=jnp.bfloat16):
    result = jax.random.normal(stream_key, extent, jnp.float32) * scale
    if len(shards) > 0:
        result = block_scale(stream_key, extent, shards, -0.22, 0.18) * result
    return jnp.clip(result, min=-reach, max=reach).astype(dtype)


def setup_inputs(seed: int = 0) -> dict:
    arg_keys = jax.random.split(jax.random.key(seed), 6)
    queries = draw_queries(jax.random.fold_in(arg_keys[5], 71), 0)
    keys_in = draw_keys_in(jax.random.fold_in(arg_keys[5], 71), 0)
    values_in = centred(arg_keys[2], (SEQS, LENGTH, HD), 1.0, 6.0, ((0, 16), (1, 32)))
    cotangent = centred(arg_keys[3], (SEQS, LENGTH, HD), 1.0, 6.0, ((0, 16), (1, 32)))
    level_slope = jnp.clip(jax.random.uniform(arg_keys[4], (HEADS,), jnp.float32, -0.4, 0.2), -0.4, 0.2)
    return dict(queries=queries, keys_in=keys_in, values_in=values_in, cotangent=cotangent, level_slope=level_slope)


LOG_TWO = math.log(2.0)

def pool_pairs(rows):
    count = rows.shape[0] // 2
    wide = rows.astype(jnp.float32).reshape(count, 2, rows.shape[1])
    return (0.5 * (wide[:, 0] + wide[:, 1])).astype(jnp.bfloat16)

def spread_pairs(grads):
    return jnp.repeat(0.5 * grads, 2, axis=0)

def pair_swap(blocks):
    groups = blocks.shape[0]
    rest = blocks.shape[1:]
    return blocks.reshape((groups // 2, 2) + rest)[:, ::-1].reshape((groups,) + rest)

def one_sequence(queries, keys_in, values_in, cotangent, level_slope):
    length, width = queries.shape
    heads = level_slope.shape[0]
    head_dim = width // heads
    scale = 1.0 / math.sqrt(head_dim)
    depth_count = (length // LEAF).bit_length() - 1
    coarse_keys = [keys_in]
    coarse_vals = [values_in]
    for level_idx in range(1, depth_count):
        coarse_keys.append(pool_pairs(coarse_keys[-1]))
        coarse_vals.append(pool_pairs(coarse_vals[-1]))
    query_f = queries.astype(jnp.float32).reshape(length, heads, head_dim)
    cot_f = cotangent.astype(jnp.float32).reshape(length, heads, head_dim)
    setups = []
    for level_idx in range(depth_count):
        if level_idx == 0:
            groups = length // (2 * LEAF)
            key_blk = keys_in.reshape(groups, 2 * LEAF, heads, head_dim)
            val_blk = values_in.reshape(groups, 2 * LEAF, heads, head_dim)
        else:
            groups = length // (LEAF * 2 ** level_idx)
            key_blk = pair_swap(coarse_keys[level_idx].reshape(groups, LEAF, heads, head_dim))
            val_blk = pair_swap(coarse_vals[level_idx].reshape(groups, LEAF, heads, head_dim))
        setups.append((groups, key_blk.astype(jnp.float32), val_blk.astype(jnp.float32), level_idx))
    score_list = []
    for groups, key_blk, val_blk, level_idx in setups:
        query_g = query_f.reshape(groups, length // groups, heads, head_dim)
        raw = jnp.einsum('gqhd,gkhd->gqhk', query_g, key_blk).reshape(length, heads, key_blk.shape[1])
        score_list.append(raw * scale + (level_idx * (LOG_TWO + level_slope))[:, None])
    scores = jnp.concatenate(score_list, axis=-1)
    top = lax.optimization_barrier(jnp.max(scores, axis=-1, keepdims=True))
    expo = jnp.exp(scores - top)
    probs = expo / lax.optimization_barrier(jnp.sum(expo, axis=-1, keepdims=True))
    probs_b = probs.astype(jnp.bfloat16).astype(jnp.float32)
    sizes = [setup[1].shape[1] for setup in setups]
    offsets = [sum(sizes[:index]) for index in range(len(sizes))]
    attended = jnp.zeros((length, heads, head_dim), jnp.float32)
    for (groups, key_blk, val_blk, level_idx), start in zip(setups, offsets):
        part = probs_b[:, :, start:start + key_blk.shape[1]].reshape(groups, length // groups, heads, key_blk.shape[1])
        attended = attended + jnp.einsum('gqhk,gkhd->gqhd', part, val_blk).reshape(length, heads, head_dim)
    delta = lax.optimization_barrier(jnp.sum(cot_f * attended, axis=-1, keepdims=True))
    dprob_list = []
    for groups, key_blk, val_blk, level_idx in setups:
        cot_g = cot_f.reshape(groups, length // groups, heads, head_dim)
        dprob_list.append(jnp.einsum('gqhd,gkhd->gqhk', cot_g, val_blk).reshape(length, heads, key_blk.shape[1]))
    dscores = probs * (jnp.concatenate(dprob_list, axis=-1) - delta)
    dscores_b = dscores.astype(jnp.bfloat16).astype(jnp.float32)
    grad_slope = jnp.zeros((heads,), jnp.float32)
    grad_query = jnp.zeros((length, heads, head_dim), jnp.float32)
    key_grads = []
    val_grads = []
    for (groups, key_blk, val_blk, level_idx), start in zip(setups, offsets):
        width_k = key_blk.shape[1]
        grad_slope = grad_slope + level_idx * lax.optimization_barrier(jnp.sum(dscores[:, :, start:start + width_k], axis=(0, 2)))
        ds_g = dscores_b[:, :, start:start + width_k].reshape(groups, length // groups, heads, width_k)
        pb_g = probs_b[:, :, start:start + width_k].reshape(groups, length // groups, heads, width_k)
        query_g = query_f.reshape(groups, length // groups, heads, head_dim)
        cot_g = cot_f.reshape(groups, length // groups, heads, head_dim)
        grad_query = grad_query + jnp.einsum('gqhk,gkhd->gqhd', ds_g, key_blk).reshape(length, heads, head_dim) * scale
        dkey = jnp.einsum('gqhk,gqhd->gkhd', ds_g, query_g) * scale
        dval = jnp.einsum('gqhk,gqhd->gkhd', pb_g, cot_g)
        if level_idx > 0:
            dkey = pair_swap(dkey)
            dval = pair_swap(dval)
        key_grads.append(dkey.reshape(-1, width))
        val_grads.append(dval.reshape(-1, width))
    for level_idx in range(depth_count - 1, 0, -1):
        key_grads[level_idx - 1] = key_grads[level_idx - 1] + spread_pairs(key_grads[level_idx])
        val_grads[level_idx - 1] = val_grads[level_idx - 1] + spread_pairs(val_grads[level_idx])
    return (grad_query.reshape(length, width).astype(jnp.bfloat16), key_grads[0].astype(jnp.bfloat16), val_grads[0].astype(jnp.bfloat16), grad_slope)

def reference(queries, keys_in, values_in, cotangent, level_slope):

    def run_one(items):
        return one_sequence(items[0], items[1], items[2], items[3], level_slope)
    grad_q, grad_k, grad_v, slopes = lax.map(run_one, (queries, keys_in, values_in, cotangent))
    return (grad_q, grad_k, grad_v, lax.optimization_barrier(jnp.sum(slopes, axis=0)))
```

```python
import math

import jax
import jax.numpy as jnp
from jax import lax
from jax.experimental import pallas as pl
from jax.experimental.pallas import tpu as pltpu
from jax.sharding import PartitionSpec as P

LOG_TWO = math.log(2.0)
HEADS = 8
HEAD_DIM = 128
WIDTH = HEADS * HEAD_DIM
TOKENS = 128
PEERS = 32
LEVELS = 8
KEYS = 144
ROWS = 304
FAR = 48
SCALE = 1.0 / math.sqrt(HEAD_DIM)
F32 = jnp.float32
BF16 = jnp.bfloat16


def iota2(rows, cols):
    row = lax.broadcasted_iota(jnp.int32, (rows, cols), 0)
    col = lax.broadcasted_iota(jnp.int32, (rows, cols), 1)
    return row, col


def mat(mask, weight):
    return jnp.where(mask, weight, 0.0).astype(BF16)


def mm(left, right, dims=((1,), (0,))):
    return lax.dot_general(left, right, (dims, ((), ())), preferred_element_type=F32)


def pooling(rows, cols):
    row, col = iota2(rows, cols)
    return mat((col >> 1) == row, 0.5)


def pool_kernel(k_ref, v_ref, l1_ref, l2_ref, l3_ref, l4_ref, slot_ref):
    me = lax.axis_index("seq")
    half = pooling(64, 128)
    l1_ref[0:64, :] = mm(half, k_ref[...]).astype(BF16)
    l1_ref[64:128, :] = mm(half, v_ref[...]).astype(BF16)
    l2 = mm(pooling(64, 128), l1_ref[...]).astype(BF16)
    l2_ref[...] = l2
    l3 = mm(pooling(32, 64), l2).astype(BF16)
    l3_ref[...] = l3
    l4 = mm(pooling(16, 32), l3).astype(BF16)
    l4_ref[...] = l4
    row, col = iota2(16, 16)
    l5 = mm(pooling(16, 16), l4).astype(BF16)
    m6 = mat((row < 8) & ((row & 3) < 2) & ((col >> 1) == ((row >> 2) * 2 + (row & 3))), 0.5)
    l6 = mm(m6, l5).astype(BF16)
    m7 = mat((row < 8) & ((row & 3) == 0) & ((col >> 1) == (row >> 1)), 0.5)
    l7 = mm(m7, l6).astype(BF16)
    b5, b6, b7 = l5[0:8], l6[0:8], l7[0:8]
    base7 = ((me >> 4) ^ 1) << 4
    base6 = ((me >> 3) ^ 1) << 3
    base5 = ((me >> 2) ^ 1) << 2
    base4 = (me >> 2) << 2
    for i in range(16):
        slot_ref[base7 + i] = b7
    for i in range(8):
        slot_ref[base6 + i] = b6
    for i in range(4):
        slot_ref[base5 + i] = b5
    for i in range(4):
        slot_ref[base4 + i] = jnp.zeros((8, WIDTH), BF16)


def far_column(me, line):
    at5 = ((((me >> 2) ^ 1) << 2) + (line >> 2)) * 8 + (line & 3)
    six = line - 16
    at6 = ((((me >> 3) ^ 1) << 3) + (six >> 1)) * 8 + (six & 1)
    at7 = ((((me >> 4) ^ 1) << 4) + (line - 32)) * 8
    return jnp.where(line < 16, at5, jnp.where(line < 32, at6, at7))


def score_kernel(
    slope_ref, q_ref, c_ref, k_ref, v_ref, l1_ref, l2_ref, r3_ref, r4a_ref, r4b_ref, r_ref,
    kf_ref, vf_ref, p_ref, d_ref, s_ref,
):
    me = lax.axis_index("seq")
    row, col = iota2(FAR, PEERS * 8)
    place = far_column(me, row)
    far = r_ref[...]
    prow, pcol = iota2(16, 16)
    for out_ref, own_ref, which in ((kf_ref, k_ref, 0), (vf_ref, v_ref, 1)):
        out_ref[0:128, :] = own_ref[...]
        out_ref[128:192, :] = l1_ref[64 * which : 64 * which + 64, :]
        out_ref[192:224, :] = l2_ref[32 * which : 32 * which + 32, :]
        out_ref[224:240, :] = r3_ref[16 * which : 16 * which + 16, :]
        first = mat((prow < 8) & (pcol == prow + 8 * which), 1.0)
        second = mat((prow >= 8) & (pcol == prow - 8 + 8 * which), 1.0)
        out_ref[240:256, :] = (mm(first, r4a_ref[...]) + mm(second, r4b_ref[...])).astype(BF16)
        out_ref[256:304, :] = mm(mat(col == place + 4 * which, 1.0), far).astype(BF16)

    lane = lax.broadcasted_iota(jnp.int32, (1, TOKENS), 1)
    quarter = lane >> 5
    lower = lane < 64

    def compact(full):
        def by_quarter(blocks):
            return jnp.where(
                quarter < 2,
                jnp.where(quarter == 0, blocks[0], blocks[1]),
                jnp.where(quarter == 2, blocks[2], blocks[3]),
            )

        zero = by_quarter([full[32 * g : 32 * g + 32] for g in range(4)])
        one = by_quarter([full[128 + 16 * (g ^ 1) : 144 + 16 * (g ^ 1)] for g in range(4)])
        two = jnp.where(lower, full[208:224], full[192:208])
        return [zero, one, two] + [full[224 + 16 * i : 240 + 16 * i] for i in range(5)]

    total = [None] * HEADS
    for h in range(HEADS):
        sl = slice(h * HEAD_DIM, (h + 1) * HEAD_DIM)
        raw = mm(kf_ref[:, sl], q_ref[:, sl], ((1,), (1,)))
        step = LOG_TWO + slope_ref[h]
        parts = [piece * SCALE + level * step for level, piece in enumerate(compact(raw))]
        scores = jnp.concatenate(parts, axis=0)
        top = jnp.max(scores, axis=0, keepdims=True)
        expo = jnp.exp(scores - top)
        probs = expo * (1.0 / jnp.sum(expo, axis=0, keepdims=True))
        probs_b = probs.astype(BF16)
        dprobs = jnp.concatenate(compact(mm(vf_ref[:, sl], c_ref[:, sl], ((1,), (1,)))), axis=0)
        delta = jnp.sum(probs_b.astype(F32) * dprobs, axis=0, keepdims=True)
        dscores = probs * (dprobs - delta)
        p_ref[h] = probs_b
        d_ref[h] = dscores.astype(BF16)
        acc = None
        for level in range(1, LEVELS):
            at = 16 + 16 * level
            term = level * (dscores[at : at + 8] + dscores[at + 8 : at + 16])
            acc = term if acc is None else acc + term
        total[h] = jnp.sum(acc, axis=0, keepdims=True)
    tile = jnp.concatenate(total, axis=0)
    for i in range(s_ref.shape[0]):
        s_ref[i] = tile


def grad_kernel(
    q_ref, c_ref, kf_ref, vf_ref, p_ref, d_ref,
    dq_ref, gk_ref, gv_ref, g3_ref, g4a_ref, g4b_ref, gf_ref,
):
    lane = lax.broadcasted_iota(jnp.int32, (1, TOKENS), 1)
    quarter = lane >> 5
    lower = lane < 64
    row, col = iota2(TOKENS, 96)
    spread = jnp.where(
        (col < 64) & (col == (row >> 1)),
        0.5,
        jnp.where((col >= 64) & (col - 64 == (row >> 2)), 0.25, 0.0),
    ).astype(BF16)

    def expand(part):
        part = part.astype(F32)
        zero, one, two, rest = part[0:32], part[32:48], part[48:64], part[64:144]
        rows = [jnp.where(quarter == g, zero, 0.0) for g in range(4)]
        rows += [jnp.where(quarter == (g ^ 1), one, 0.0) for g in range(4)]
        rows += [jnp.where(lower, 0.0, two), jnp.where(lower, two, 0.0), rest]
        return jnp.concatenate(rows, axis=0).astype(BF16)

    for h in range(HEADS):
        sl = slice(h * HEAD_DIM, (h + 1) * HEAD_DIM)
        d_full = expand(d_ref[h])
        p_full = expand(p_ref[h])
        dq_ref[:, sl] = (mm(d_full, kf_ref[:, sl], ((0,), (0,))) * SCALE).astype(BF16)
        dk = mm(d_full, q_ref[:, sl]) * SCALE
        dv = mm(p_full, c_ref[:, sl])
        gk_ref[:, sl] = dk[0:128] + mm(spread, dk[128:224].astype(BF16))
        gv_ref[:, sl] = dv[0:128] + mm(spread, dv[128:224].astype(BF16))
        g3_ref[0:16, sl] = dk[224:240].astype(BF16)
        g3_ref[16:32, sl] = dv[224:240].astype(BF16)
        g4a_ref[:, sl] = jnp.concatenate([dk[240:248], dv[240:248]], axis=0).astype(BF16)
        g4b_ref[:, sl] = jnp.concatenate([dk[248:256], dv[248:256]], axis=0).astype(BF16)
        gf_ref[0:FAR, sl] = dk[256:304].astype(BF16)
        gf_ref[FAR : 2 * FAR, sl] = dv[256:304].astype(BF16)


def pack_kernel(gf_ref, s_ref, out_ref):
    me = lax.axis_index("seq")
    row, col = iota2(PEERS * 8, 2 * FAR)
    is_key = col < FAR
    place = far_column(me, jnp.where(is_key, col, col - FAR)) + jnp.where(is_key, 0, 4)
    out_ref[:, 0:WIDTH] = mm(mat(row == place, 1.0), gf_ref[...]).astype(BF16)
    value = jnp.sum(jnp.sum(s_ref[...], axis=0), axis=1, keepdims=True)
    high = value.astype(BF16).astype(F32)
    rest = value - high
    middle = rest.astype(BF16).astype(F32)
    low = rest - middle
    lane = lax.broadcasted_iota(jnp.int32, (HEADS, 128), 1)
    tile = jnp.where(
        lane == 0, high, jnp.where(lane == 1, middle, jnp.where(lane == 2, low, 0.0))
    )
    out_ref[:, WIDTH:] = jnp.concatenate([tile] * PEERS, axis=0).astype(BF16)


def final_kernel(gk_ref, gv_ref, r3_ref, r4a_ref, r4b_ref, r_ref, ok_ref, ov_ref, os_ref):
    me = lax.axis_index("seq")
    row, col = iota2(TOKENS, PEERS * 8)
    apart = (col >> 3) ^ me
    line = col & 7
    shift = jnp.where(apart >= 16, 7, jnp.where(apart >= 8, 6, 5))
    weight = jnp.where(
        apart >= 16, 2.0**-7, jnp.where(apart >= 8, 2.0**-6, jnp.where(apart >= 4, 2.0**-5, 0.0))
    )
    covers = lax.shift_right_logical(row, shift)
    row3, col3 = iota2(TOKENS, 32)
    row4, col4 = iota2(TOKENS, 16)
    for out_ref, own_ref, which in ((ok_ref, gk_ref, 0), (ov_ref, gv_ref, 1)):
        total = own_ref[...]
        total += mm(mat(covers + 4 * which == line, weight), r_ref[:, 0:WIDTH])
        total += mm(mat((row3 >> 3) + 16 * which == col3, 2.0**-3), r3_ref[...])
        both = mat((row4 >> 4) + 8 * which == col4, 2.0**-4)
        total += mm(both, r4a_ref[...]) + mm(both, r4b_ref[...])
        out_ref[...] = total.astype(BF16)
    slopes = r_ref[:, WIDTH:].astype(F32).reshape(PEERS, HEADS, 128)
    value = jnp.sum(jnp.sum(slopes, axis=0), axis=1, keepdims=True)
    srow, scol = iota2(HEADS, 128)
    line = jnp.sum(jnp.where(srow == scol, value, 0.0), axis=0, keepdims=True)
    os_ref[...] = line[:, 0:HEADS]


def call(kernel, outs, ins, flops=0, scalars=0):
    moved = sum(math.prod(s) * 2 for s, _ in outs)
    return pl.pallas_call(
        kernel,
        out_shape=[jax.ShapeDtypeStruct(s, t) for s, t in outs],
        in_specs=[pl.BlockSpec(memory_space=pltpu.SMEM)] * scalars
        + [pl.BlockSpec(memory_space=pltpu.VMEM)] * (len(ins) - scalars),
        out_specs=[pl.BlockSpec(memory_space=pltpu.VMEM)] * len(outs),
        compiler_params=pltpu.CompilerParams(vmem_limit_bytes=32 * 1024 * 1024),
        cost_estimate=pl.CostEstimate(flops=flops, bytes_accessed=2 * moved, transcendentals=0),
    )(*ins)


def swap(block, apart):
    return lax.ppermute(block, "seq", [(i, i ^ apart) for i in range(PEERS)])


def exchange(slots):
    width = slots.shape[-1]
    back = lax.all_to_all(slots.reshape(PEERS, 8, width), "seq", 0, 0)
    return back.reshape(PEERS * 8, width)


def per_device(queries, keys_in, values_in, cotangent, level_slope):
    q, k, v, c = queries[0], keys_in[0], values_in[0], cotangent[0]
    wide = WIDTH
    l1, l2, l3, l4, slots = call(
        pool_kernel,
        [((128, wide), BF16), ((64, wide), BF16), ((32, wide), BF16), ((16, wide), BF16),
         ((PEERS, 8, wide), BF16)],
        (k, v),
    )
    far = exchange(slots)
    near3 = swap(l3, 1)
    near4a = swap(l4, 2)
    near4b = swap(l4, 3)
    groups = lax.axis_size("dp")
    kf, vf, probs, dscores, slopes = call(
        score_kernel,
        [((ROWS, wide), BF16), ((ROWS, wide), BF16), ((HEADS, KEYS, TOKENS), BF16),
         ((HEADS, KEYS, TOKENS), BF16), ((groups, HEADS, 128), F32)],
        (level_slope, q, c, k, v, l1, l2, near3, near4a, near4b, far),
        scalars=1,
    )
    slopes = lax.all_to_all(slopes, "dp", 0, 0)
    dq, gk, gv, g3, g4a, g4b, gf = call(
        grad_kernel,
        [((TOKENS, wide), BF16), ((TOKENS, wide), F32), ((TOKENS, wide), F32), ((32, wide), BF16),
         ((16, wide), BF16), ((16, wide), BF16), ((2 * FAR, wide), BF16)],
        (q, c, kf, vf, probs, dscores),
    )
    (packed,) = call(pack_kernel, [((PEERS * 8, wide + 128), BF16)], (gf, slopes))
    far = exchange(packed)
    near3 = swap(g3, 1)
    near4a = swap(g4a, 2)
    near4b = swap(g4b, 3)
    dk, dv, ds = call(
        final_kernel,
        [((TOKENS, wide), BF16), ((TOKENS, wide), BF16), ((1, HEADS), F32)],
        (gk, gv, near3, near4a, near4b, far),
    )
    return dq[None], dk[None], dv[None], ds.reshape(HEADS)


def solution(mesh):
    row = P("dp", "seq", None)
    return jax.shard_map(
        per_device,
        mesh=mesh,
        in_specs=(row, row, row, row, P()),
        out_specs=(row, row, row, P()),
        check_vma=False,
    )
```

```python
import math

import jax
import jax.numpy as jnp
from jax import lax
from jax.experimental import pallas as pl
from jax.experimental.pallas import tpu as pltpu
from jax.sharding import PartitionSpec as P

LOG_TWO = math.log(2.0)
HEADS = 8
HEAD_DIM = 128
WIDTH = HEADS * HEAD_DIM
TOKENS = 128
PEERS = 32
LEVELS = 8
KEYS = 144
FAR = 48
SCALE = 1.0 / math.sqrt(HEAD_DIM)
LONG = 1 << 28
F32 = jnp.float32
BF16 = jnp.bfloat16


def iota2(rows, cols):
    row = lax.broadcasted_iota(jnp.int32, (rows, cols), 0)
    col = lax.broadcasted_iota(jnp.int32, (rows, cols), 1)
    return row, col


def mat(mask, weight):
    return jnp.where(mask, weight, 0.0).astype(BF16)


def mm(left, right, dims=((1,), (0,))):
    return lax.dot_general(left, right, (dims, ((), ())), preferred_element_type=F32)


def pooling(rows, cols):
    row, col = iota2(rows, cols)
    return mat((col >> 1) == row, 0.5)


def three_parts(value):
    high = value.astype(BF16).astype(F32)
    rest = value - high
    middle = rest.astype(BF16).astype(F32)
    return high, middle, rest - middle


LOCAL = 224
STEP = 2 * LOCAL
REMOTE = 80
PROBS = 2 * REMOTE
DSCORES = PROBS + KEYS


def pool_kernel(k_hbm, v_hbm, slope_hbm, kv_ref, l3_ref, l4_ref, slot_ref, slope_ref, sems):
    me = lax.axis_index("seq")
    fetch_k = pltpu.make_async_copy(k_hbm, kv_ref.at[pl.ds(0, TOKENS)], sems.at[0])
    fetch_v = pltpu.make_async_copy(v_hbm, kv_ref.at[pl.ds(LOCAL, TOKENS)], sems.at[1])
    fetch_slope = pltpu.make_async_copy(slope_hbm, slope_ref, sems.at[2])
    fetch_k.start()
    fetch_v.start()
    fetch_slope.start()
    half = pooling(64, 128)
    quarter = pooling(32, 64)
    fetch_slope.wait()
    line = lax.broadcasted_iota(jnp.int32, (16, HEAD_DIM), 0)
    for h in range(HEADS):
        high, middle, low = three_parts(jnp.full((16, HEAD_DIM), LOG_TWO + slope_ref[h], F32))
        part = jnp.where(line == 0, high, jnp.where(line == 1, middle, jnp.where(line == 2, low, 0.0)))
        kv_ref[STEP : STEP + 16, h * HEAD_DIM : (h + 1) * HEAD_DIM] = part.astype(BF16)
    l2 = []
    for fetch, at in ((fetch_k, 0), (fetch_v, LOCAL)):
        fetch.wait()
        one = mm(half, kv_ref[at : at + 128, :]).astype(BF16)
        kv_ref[at + 128 : at + 192, :] = one
        two = mm(quarter, one).astype(BF16)
        kv_ref[at + 192 : at + 224, :] = two
        l2.append(two)
    l3 = mm(quarter, jnp.concatenate(l2, axis=0)).astype(BF16)
    l3_ref[...] = l3
    l4 = mm(pooling(16, 32), l3).astype(BF16)
    l4_ref[...] = l4
    row, col = iota2(16, 16)
    l5 = mm(pooling(16, 16), l4).astype(BF16)
    m6 = mat((row < 8) & ((row & 3) < 2) & ((col >> 1) == ((row >> 2) * 2 + (row & 3))), 0.5)
    l6 = mm(m6, l5).astype(BF16)
    m7 = mat((row < 8) & ((row & 3) == 0) & ((col >> 1) == (row >> 1)), 0.5)
    l7 = mm(m7, l6).astype(BF16)
    b5, b6, b7 = l5[0:8], l6[0:8], l7[0:8]
    base7 = ((me >> 4) ^ 1) << 4
    base6 = ((me >> 3) ^ 1) << 3
    base5 = ((me >> 2) ^ 1) << 2
    base4 = (me >> 2) << 2
    for i in range(16):
        slot_ref[base7 + i] = b7
    for i in range(8):
        slot_ref[base6 + i] = b6
    for i in range(4):
        slot_ref[base5 + i] = b5
    for i in range(4):
        slot_ref[base4 + i] = jnp.zeros((8, WIDTH), BF16)


def far_column(me, line):
    at5 = ((((me >> 2) ^ 1) << 2) + (line >> 2)) * 8 + (line & 3)
    six = line - 16
    at6 = ((((me >> 3) ^ 1) << 3) + (six >> 1)) * 8 + (six & 1)
    at7 = ((((me >> 4) ^ 1) << 4) + (line - 32)) * 8
    return jnp.where(line < 16, at5, jnp.where(line < 32, at6, at7))


def local_kernel(q_hbm, c_hbm, kv_ref, qc_ref, s_ref, sems):
    fetch_q = pltpu.make_async_copy(q_hbm, qc_ref.at[pl.ds(0, TOKENS)], sems.at[0])
    fetch_c = pltpu.make_async_copy(c_hbm, qc_ref.at[pl.ds(TOKENS, TOKENS)], sems.at[1])
    fetch_q.start()
    fetch_c.start()
    lane = lax.broadcasted_iota(jnp.int32, (1, TOKENS), 1)
    quarter = lane >> 5
    lower = lane < 64


    def compact(full):
        def by_quarter(blocks):
            return jnp.where(
                quarter < 2,
                jnp.where(quarter == 0, blocks[0], blocks[1]),
                jnp.where(quarter == 2, blocks[2], blocks[3]),
            )

        zero = by_quarter([full[32 * g : 32 * g + 32] for g in range(4)])
        one = by_quarter([full[128 + 16 * (g ^ 1) : 144 + 16 * (g ^ 1)] for g in range(4)])
        two = jnp.where(lower, full[208:224], full[192:208])
        return zero, one, two

    step_all = jnp.sum(kv_ref[STEP : STEP + 16, :].astype(F32), axis=0, keepdims=True)
    for which, fetch in enumerate((fetch_q, fetch_c)):
        fetch.wait()
        for h in range(HEADS):
            sl = slice(h * HEAD_DIM, (h + 1) * HEAD_DIM)
            keys = kv_ref[LOCAL * which : LOCAL * which + LOCAL, sl]
            raw = mm(keys, qc_ref[TOKENS * which : TOKENS * which + TOKENS, sl], ((1,), (1,)))
            zero, one, two = compact(raw)
            if which == 0:
                step = step_all[:, sl]
                zero, one, two = zero * SCALE, one * SCALE + step, two * SCALE + 2 * step
            s_ref[64 * which : 64 * which + 64, sl] = jnp.concatenate([zero, one, two], axis=0)


def score_kernel(kv_ref, qc_ref, near_ref, r3_ref, r4a_ref, r4b_ref, r_ref, w_ref, s_ref):
    me = lax.axis_index("seq")
    row, col = iota2(FAR, PEERS * 8)
    place = far_column(me, row)
    far = r_ref[...]
    prow, pcol = iota2(16, 16)
    for which in range(2):
        at = REMOTE * which
        w_ref[at : at + 16, :] = r3_ref[16 * which : 16 * which + 16, :]
        first = mat((prow < 8) & (pcol == prow + 8 * which), 1.0)
        second = mat((prow >= 8) & (pcol == prow - 8 + 8 * which), 1.0)
        four = mm(first, r4a_ref[...]) + mm(second, r4b_ref[...])
        w_ref[at + 16 : at + 32, :] = four.astype(BF16)
        w_ref[at + 32 : at + 80, :] = mm(mat(col == place + 4 * which, 1.0), far).astype(BF16)
    step_all = jnp.sum(kv_ref[STEP : STEP + 16, :].astype(F32), axis=0, keepdims=True)
    total = [None] * HEADS
    for h in range(HEADS):
        sl = slice(h * HEAD_DIM, (h + 1) * HEAD_DIM)
        raw = mm(w_ref[0:REMOTE, sl], qc_ref[0:TOKENS, sl], ((1,), (1,)))
        step = step_all[:, sl]
        parts = [near_ref[0:64, sl]]
        parts += [raw[16 * i : 16 * i + 16] * SCALE + (i + 3) * step for i in range(5)]
        scores = jnp.concatenate(parts, axis=0)
        top = jnp.max(scores, axis=0, keepdims=True)
        expo = jnp.exp(scores - top)
        probs = expo * (1.0 / jnp.sum(expo, axis=0, keepdims=True))
        probs_b = probs.astype(BF16)
        raw = mm(w_ref[REMOTE : 2 * REMOTE, sl], qc_ref[TOKENS : 2 * TOKENS, sl], ((1,), (1,)))
        dprobs = jnp.concatenate([near_ref[64:128, sl], raw], axis=0)
        delta = jnp.sum(probs_b.astype(F32) * dprobs, axis=0, keepdims=True)
        dscores = probs * (dprobs - delta)
        w_ref[PROBS : PROBS + KEYS, sl] = probs_b
        w_ref[DSCORES : DSCORES + KEYS, sl] = dscores.astype(BF16)
        acc = None
        for level in range(1, LEVELS):
            at = 16 + 16 * level
            term = level * (dscores[at : at + 8] + dscores[at + 8 : at + 16])
            acc = term if acc is None else acc + term
        total[h] = jnp.sum(acc, axis=0, keepdims=True)
    tile = jnp.concatenate(total, axis=0)
    for i in range(s_ref.shape[0]):
        s_ref[i] = tile


def grad_kernel(kv_ref, qc_ref, w_ref, dq_ref, gk_ref, gv_ref, g3_ref, g4a_ref, g4b_ref, slot_ref, gf_ref):
    me = lax.axis_index("seq")
    lane = lax.broadcasted_iota(jnp.int32, (1, TOKENS), 1)
    quarter = lane >> 5
    lower = lane < 64

    srow, scol = iota2(TOKENS, 96)
    spread = jnp.where(
        (scol < 64) & (scol == (srow >> 1)),
        0.5,
        jnp.where((scol >= 64) & (scol - 64 == (srow >> 2)), 0.25, 0.0),
    ).astype(BF16)

    def expand(part):
        part = part.astype(F32)
        zero, one, two = part[0:32], part[32:48], part[48:64]
        rows = [jnp.where(quarter == g, zero, 0.0) for g in range(4)]
        rows += [jnp.where(quarter == (g ^ 1), one, 0.0) for g in range(4)]
        rows += [jnp.where(lower, 0.0, two), jnp.where(lower, two, 0.0)]
        return jnp.concatenate(rows, axis=0).astype(BF16)

    for h in range(HEADS):
        sl = slice(h * HEAD_DIM, (h + 1) * HEAD_DIM)
        q, c = qc_ref[0:TOKENS, sl], qc_ref[TOKENS : 2 * TOKENS, sl]
        d_near = expand(w_ref[DSCORES : DSCORES + 64, sl])
        p_near = expand(w_ref[PROBS : PROBS + 64, sl])
        d_far = w_ref[DSCORES + 64 : DSCORES + KEYS, sl]
        p_far = w_ref[PROBS + 64 : PROBS + KEYS, sl]
        dq = mm(d_near, kv_ref[0:LOCAL, sl], ((0,), (0,))) + mm(d_far, w_ref[0:REMOTE, sl], ((0,), (0,)))
        dq_ref[:, sl] = (dq * SCALE).astype(BF16)
        dk = mm(d_near, q) * SCALE
        dv = mm(p_near, c)
        gk_ref[:, sl] = dk[0:128] + mm(spread, dk[128:224].astype(BF16))
        gv_ref[:, sl] = dv[0:128] + mm(spread, dv[128:224].astype(BF16))
        dk = mm(d_far, q) * SCALE
        dv = mm(p_far, c)
        g3_ref[0:16, sl] = dk[0:16].astype(BF16)
        g3_ref[16:32, sl] = dv[0:16].astype(BF16)
        g4a_ref[:, sl] = jnp.concatenate([dk[16:24], dv[16:24]], axis=0).astype(BF16)
        g4b_ref[:, sl] = jnp.concatenate([dk[24:32], dv[24:32]], axis=0).astype(BF16)
        gf_ref[0:FAR, sl] = dk[32:80].astype(BF16)
        gf_ref[FAR : 2 * FAR, sl] = dv[32:80].astype(BF16)
    row, col = iota2(PEERS * 8, 2 * FAR)
    is_key = col < FAR
    place = far_column(me, jnp.where(is_key, col, col - FAR)) + jnp.where(is_key, 0, 4)
    slot_ref[:, 0:WIDTH] = mm(mat(row == place, 1.0), gf_ref[...]).astype(BF16)
    slot_ref[:, WIDTH:] = jnp.zeros((PEERS * 8, 128), BF16)


def slope_kernel(s_ref, slot_in, slot_out, tile_ref, sem):
    value = jnp.sum(jnp.sum(s_ref[...], axis=0), axis=1, keepdims=True)
    high, middle, low = three_parts(value)
    lane = lax.broadcasted_iota(jnp.int32, (HEADS, 128), 1)
    tile = jnp.where(
        lane == 0, high, jnp.where(lane == 1, middle, jnp.where(lane == 2, low, 0.0))
    )
    tile_ref[...] = jnp.concatenate([tile] * PEERS, axis=0).astype(BF16)
    put = pltpu.make_async_copy(tile_ref, slot_out.at[:, pl.ds(WIDTH, 128)], sem)
    put.start()
    put.wait()


def final_kernel(gk_ref, gv_ref, r3_ref, r4a_ref, r4b_ref, r_ref, ok_ref, ov_ref, os_ref):
    me = lax.axis_index("seq")
    row, col = iota2(TOKENS, PEERS * 8)
    apart = (col >> 3) ^ me
    line = col & 7
    shift = jnp.where(apart >= 16, 7, jnp.where(apart >= 8, 6, 5))
    weight = jnp.where(
        apart >= 16, 2.0**-7, jnp.where(apart >= 8, 2.0**-6, jnp.where(apart >= 4, 2.0**-5, 0.0))
    )
    covers = lax.shift_right_logical(row, shift)
    row3, col3 = iota2(TOKENS, 32)
    row4, col4 = iota2(TOKENS, 16)
    for out_ref, own_ref, which in ((ok_ref, gk_ref, 0), (ov_ref, gv_ref, 1)):
        total = own_ref[...]
        total += mm(mat(covers + 4 * which == line, weight), r_ref[:, 0:WIDTH])
        total += mm(mat((row3 >> 3) + 16 * which == col3, 2.0**-3), r3_ref[...])
        both = mat((row4 >> 4) + 8 * which == col4, 2.0**-4)
        total += mm(both, r4a_ref[...]) + mm(both, r4b_ref[...])
        out_ref[...] = total.astype(BF16)
    slopes = r_ref[:, WIDTH:].astype(F32).reshape(PEERS, HEADS, 128)
    value = jnp.sum(jnp.sum(slopes, axis=0), axis=1, keepdims=True)
    srow, scol = iota2(HEADS, 128)
    line = jnp.sum(jnp.where(srow == scol, value, 0.0), axis=0, keepdims=True)
    os_ref[...] = line[:, 0:HEADS]


def call(kernel, outs, ins, places=None, out_places=None, scratch=(), cost=1 << 20, alias=None, vmem=12):
    places = places or [pltpu.VMEM] * len(ins)
    out_places = out_places or [pltpu.VMEM] * len(outs)
    return pl.pallas_call(
        kernel,
        out_shape=[jax.ShapeDtypeStruct(s, t) for s, t in outs],
        in_specs=[pl.BlockSpec(memory_space=place) for place in places],
        out_specs=[pl.BlockSpec(memory_space=place) for place in out_places],
        scratch_shapes=list(scratch),
        input_output_aliases=alias or {},
        compiler_params=pltpu.CompilerParams(vmem_limit_bytes=vmem * 1024 * 1024),
        cost_estimate=pl.CostEstimate(flops=0, bytes_accessed=cost, transcendentals=0),
    )(*ins)


def swap(block, apart):
    return lax.ppermute(block, "seq", [(i, i ^ apart) for i in range(PEERS)])


def exchange(slots):
    width = slots.shape[-1]
    back = lax.all_to_all(slots.reshape(PEERS, 8, width), "seq", 0, 0)
    return back.reshape(PEERS * 8, width)


def per_device(queries, keys_in, values_in, cotangent, level_slope):
    q, k, v, c = queries[0], keys_in[0], values_in[0], cotangent[0]
    wide = WIDTH
    kv, l3, l4, slots = call(
        pool_kernel,
        [((STEP + 16, wide), BF16), ((32, wide), BF16), ((16, wide), BF16), ((PEERS, 8, wide), BF16)],
        (k, v, level_slope),
        [pl.ANY] * 3,
        scratch=[pltpu.SMEM((HEADS,), F32), pltpu.SemaphoreType.DMA((3,))],
        vmem=58,
    )
    far = exchange(slots)
    near3 = swap(l3, 1)
    near4a = swap(l4, 2)
    near4b = swap(l4, 3)
    qc, near = call(
        local_kernel,
        [((2 * TOKENS, wide), BF16), ((128, wide), F32)],
        (q, c, kv),
        [pl.ANY, pl.ANY, pltpu.VMEM],
        scratch=[pltpu.SemaphoreType.DMA((2,))],
        cost=LONG,
    )
    groups = lax.axis_size("dp")
    work, slopes = call(
        score_kernel,
        [((DSCORES + KEYS, wide), BF16), ((groups, HEADS, 128), F32)],
        (kv, qc, near, near3, near4a, near4b, far),
    )
    slopes = lax.all_to_all(slopes, "dp", 0, 0)
    dq, gk, gv, g3, g4a, g4b, slots = call(
        grad_kernel,
        [((TOKENS, wide), BF16), ((TOKENS, wide), F32), ((TOKENS, wide), F32), ((32, wide), BF16),
         ((16, wide), BF16), ((16, wide), BF16), ((PEERS * 8, wide + 128), BF16)],
        (kv, qc, work),
        scratch=[pltpu.VMEM((2 * FAR, wide), BF16)],
    )
    (slots,) = call(
        slope_kernel,
        [((PEERS * 8, wide + 128), BF16)],
        (slopes, slots),
        [pltpu.VMEM, pl.ANY],
        [pl.ANY],
        [pltpu.VMEM((PEERS * 8, 128), BF16), pltpu.SemaphoreType.DMA(())],
        alias={1: 0},
    )
    far = exchange(slots)
    near3 = swap(g3, 1)
    near4a = swap(g4a, 2)
    near4b = swap(g4b, 3)
    dk, dv, ds = call(
        final_kernel,
        [((TOKENS, wide), BF16), ((TOKENS, wide), BF16), ((1, HEADS), F32)],
        (gk, gv, near3, near4a, near4b, far),
    )
    return dq[None], dk[None], dv[None], ds.reshape(HEADS)


def solution(mesh):
    row = P("dp", "seq", None)
    return jax.shard_map(
        per_device,
        mesh=mesh,
        in_specs=(row, row, row, row, P()),
        out_specs=(row, row, row, P()),
        check_vma=False,
    )
```

```python
import math

import jax
import jax.numpy as jnp
from jax import lax
from jax.experimental import pallas as pl
from jax.experimental.pallas import tpu as pltpu
from jax.sharding import PartitionSpec as P

LOG_TWO = math.log(2.0)
HEADS = 8
HEAD_DIM = 128
WIDTH = HEADS * HEAD_DIM
TOKENS = 128
PEERS = 32
LEVELS = 8
KEYS = 144
FAR = 48
SCALE = 1.0 / math.sqrt(HEAD_DIM)
LONG = 1 << 28
F32 = jnp.float32
BF16 = jnp.bfloat16


def iota2(rows, cols):
    row = lax.broadcasted_iota(jnp.int32, (rows, cols), 0)
    col = lax.broadcasted_iota(jnp.int32, (rows, cols), 1)
    return row, col


def mat(mask, weight):
    return jnp.where(mask, weight, 0.0).astype(BF16)


def mm(left, right, dims=((1,), (0,))):
    return lax.dot_general(left, right, (dims, ((), ())), preferred_element_type=F32)


def pooling(rows, cols):
    row, col = iota2(rows, cols)
    return mat((col >> 1) == row, 0.5)


def three_parts(value):
    high = value.astype(BF16).astype(F32)
    rest = value - high
    middle = rest.astype(BF16).astype(F32)
    return high, middle, rest - middle


LOCAL = 224
COARSE = 96
STEP = 2 * COARSE
REMOTE = 80
PROBS = 2 * REMOTE
DSCORES = PROBS + KEYS
QUERY = LOCAL
COTANGENT = LOCAL + TOKENS
STEPS = LOCAL + 2 * TOKENS


def pool_kernel(
    k_hbm, v_hbm, slope_hbm, low_ref, l3_ref, l4_ref, slot_ref, k_ref, v_ref, slope_ref, sems
):
    me = lax.axis_index("seq")
    fetch_k = pltpu.make_async_copy(k_hbm, k_ref, sems.at[0])
    fetch_v = pltpu.make_async_copy(v_hbm, v_ref, sems.at[1])
    fetch_slope = pltpu.make_async_copy(slope_hbm, slope_ref, sems.at[2])
    fetch_k.start()
    fetch_v.start()
    fetch_slope.start()
    half = pooling(64, 128)
    quarter = pooling(32, 64)
    fetch_slope.wait()
    line = lax.broadcasted_iota(jnp.int32, (16, HEAD_DIM), 0)
    for h in range(HEADS):
        high, middle, low = three_parts(jnp.full((16, HEAD_DIM), LOG_TWO + slope_ref[h], F32))
        part = jnp.where(line == 0, high, jnp.where(line == 1, middle, jnp.where(line == 2, low, 0.0)))
        low_ref[STEP : STEP + 16, h * HEAD_DIM : (h + 1) * HEAD_DIM] = part.astype(BF16)
    l2 = []
    for fetch, held, at in ((fetch_k, k_ref, 0), (fetch_v, v_ref, COARSE)):
        fetch.wait()
        one = mm(half, held[...]).astype(BF16)
        low_ref[at : at + 64, :] = one
        two = mm(quarter, one).astype(BF16)
        low_ref[at + 64 : at + 96, :] = two
        l2.append(two)
    l3 = mm(quarter, jnp.concatenate(l2, axis=0)).astype(BF16)
    l3_ref[...] = l3
    l4 = mm(pooling(16, 32), l3).astype(BF16)
    l4_ref[...] = l4
    row, col = iota2(16, 16)
    l5 = mm(pooling(16, 16), l4).astype(BF16)
    m6 = mat((row < 8) & ((row & 3) < 2) & ((col >> 1) == ((row >> 2) * 2 + (row & 3))), 0.5)
    l6 = mm(m6, l5).astype(BF16)
    m7 = mat((row < 8) & ((row & 3) == 0) & ((col >> 1) == (row >> 1)), 0.5)
    l7 = mm(m7, l6).astype(BF16)
    b5, b6, b7 = l5[0:8], l6[0:8], l7[0:8]
    base7 = ((me >> 4) ^ 1) << 4
    base6 = ((me >> 3) ^ 1) << 3
    base5 = ((me >> 2) ^ 1) << 2
    base4 = (me >> 2) << 2
    for i in range(16):
        slot_ref[base7 + i] = b7
    for i in range(8):
        slot_ref[base6 + i] = b6
    for i in range(4):
        slot_ref[base5 + i] = b5
    for i in range(4):
        slot_ref[base4 + i] = jnp.zeros((8, WIDTH), BF16)


def far_column(me, line):
    at5 = ((((me >> 2) ^ 1) << 2) + (line >> 2)) * 8 + (line & 3)
    six = line - 16
    at6 = ((((me >> 3) ^ 1) << 3) + (six >> 1)) * 8 + (six & 1)
    at7 = ((((me >> 4) ^ 1) << 4) + (line - 32)) * 8
    return jnp.where(line < 16, at5, jnp.where(line < 32, at6, at7))


def local_kernel(q_hbm, c_hbm, k_hbm, v_hbm, low_ref, loc_ref, s_ref, v_ref, sems):
    moves = (
        (k_hbm, loc_ref.at[pl.ds(0, TOKENS)]),
        (q_hbm, loc_ref.at[pl.ds(QUERY, TOKENS)]),
        (v_hbm, v_ref.at[pl.ds(0, TOKENS)]),
        (c_hbm, loc_ref.at[pl.ds(COTANGENT, TOKENS)]),
    )
    fetches = [pltpu.make_async_copy(a, b, sems.at[i]) for i, (a, b) in enumerate(moves)]
    for fetch in fetches:
        fetch.start()
    loc_ref[TOKENS:LOCAL, :] = low_ref[0:COARSE, :]
    v_ref[TOKENS:LOCAL, :] = low_ref[COARSE : 2 * COARSE, :]
    loc_ref[STEPS : STEPS + 16, :] = low_ref[STEP : STEP + 16, :]
    lane = lax.broadcasted_iota(jnp.int32, (1, TOKENS), 1)
    quarter = lane >> 5
    lower = lane < 64


    def compact(full):
        def by_quarter(blocks):
            return jnp.where(
                quarter < 2,
                jnp.where(quarter == 0, blocks[0], blocks[1]),
                jnp.where(quarter == 2, blocks[2], blocks[3]),
            )

        zero = by_quarter([full[32 * g : 32 * g + 32] for g in range(4)])
        one = by_quarter([full[128 + 16 * (g ^ 1) : 144 + 16 * (g ^ 1)] for g in range(4)])
        two = jnp.where(lower, full[208:224], full[192:208])
        return zero, one, two

    step_all = jnp.sum(low_ref[STEP : STEP + 16, :].astype(F32), axis=0, keepdims=True)
    for which, (held, at) in enumerate(((loc_ref, QUERY), (v_ref, COTANGENT))):
        fetches[2 * which].wait()
        fetches[2 * which + 1].wait()
        for h in range(HEADS):
            sl = slice(h * HEAD_DIM, (h + 1) * HEAD_DIM)
            raw = mm(held[0:LOCAL, sl], loc_ref[at : at + TOKENS, sl], ((1,), (1,)))
            zero, one, two = compact(raw)
            if which == 0:
                step = step_all[:, sl]
                zero, one, two = zero * SCALE, one * SCALE + step, two * SCALE + 2 * step
            s_ref[64 * which : 64 * which + 64, sl] = jnp.concatenate([zero, one, two], axis=0)


def score_kernel(loc_ref, near_ref, r3_ref, r4a_ref, r4b_ref, r_ref, w_ref, s_ref):
    me = lax.axis_index("seq")
    row, col = iota2(FAR, PEERS * 8)
    place = far_column(me, row)
    far = r_ref[...]
    prow, pcol = iota2(16, 16)
    for which in range(2):
        at = REMOTE * which
        w_ref[at : at + 16, :] = r3_ref[16 * which : 16 * which + 16, :]
        first = mat((prow < 8) & (pcol == prow + 8 * which), 1.0)
        second = mat((prow >= 8) & (pcol == prow - 8 + 8 * which), 1.0)
        four = mm(first, r4a_ref[...]) + mm(second, r4b_ref[...])
        w_ref[at + 16 : at + 32, :] = four.astype(BF16)
        w_ref[at + 32 : at + 80, :] = mm(mat(col == place + 4 * which, 1.0), far).astype(BF16)
    step_all = jnp.sum(loc_ref[STEPS : STEPS + 16, :].astype(F32), axis=0, keepdims=True)
    total = [None] * HEADS
    for h in range(HEADS):
        sl = slice(h * HEAD_DIM, (h + 1) * HEAD_DIM)
        raw = mm(w_ref[0:REMOTE, sl], loc_ref[QUERY : QUERY + TOKENS, sl], ((1,), (1,)))
        step = step_all[:, sl]
        parts = [near_ref[0:64, sl]]
        parts += [raw[16 * i : 16 * i + 16] * SCALE + (i + 3) * step for i in range(5)]
        scores = jnp.concatenate(parts, axis=0)
        top = jnp.max(scores, axis=0, keepdims=True)
        expo = jnp.exp(scores - top)
        probs = expo * (1.0 / jnp.sum(expo, axis=0, keepdims=True))
        probs_b = probs.astype(BF16)
        raw = mm(w_ref[REMOTE : 2 * REMOTE, sl], loc_ref[COTANGENT : COTANGENT + TOKENS, sl], ((1,), (1,)))
        dprobs = jnp.concatenate([near_ref[64:128, sl], raw], axis=0)
        delta = jnp.sum(probs_b.astype(F32) * dprobs, axis=0, keepdims=True)
        dscores = probs * (dprobs - delta)
        w_ref[PROBS : PROBS + KEYS, sl] = probs_b
        w_ref[DSCORES : DSCORES + KEYS, sl] = dscores.astype(BF16)
        acc = None
        for level in range(1, LEVELS):
            at = 16 + 16 * level
            term = level * (dscores[at : at + 8] + dscores[at + 8 : at + 16])
            acc = term if acc is None else acc + term
        total[h] = jnp.sum(acc, axis=0, keepdims=True)
    tile = jnp.concatenate(total, axis=0)
    for i in range(s_ref.shape[0]):
        s_ref[i] = tile


def grad_kernel(loc_ref, w_ref, dq_ref, gk_ref, gv_ref, g3_ref, g4a_ref, g4b_ref, slot_ref, gf_ref):
    me = lax.axis_index("seq")
    lane = lax.broadcasted_iota(jnp.int32, (1, TOKENS), 1)
    quarter = lane >> 5
    lower = lane < 64

    srow, scol = iota2(TOKENS, 96)
    spread = jnp.where(
        (scol < 64) & (scol == (srow >> 1)),
        0.5,
        jnp.where((scol >= 64) & (scol - 64 == (srow >> 2)), 0.25, 0.0),
    ).astype(BF16)

    def expand(part):
        part = part.astype(F32)
        zero, one, two = part[0:32], part[32:48], part[48:64]
        rows = [jnp.where(quarter == g, zero, 0.0) for g in range(4)]
        rows += [jnp.where(quarter == (g ^ 1), one, 0.0) for g in range(4)]
        rows += [jnp.where(lower, 0.0, two), jnp.where(lower, two, 0.0)]
        return jnp.concatenate(rows, axis=0).astype(BF16)

    for h in range(HEADS):
        sl = slice(h * HEAD_DIM, (h + 1) * HEAD_DIM)
        q, c = loc_ref[QUERY : QUERY + TOKENS, sl], loc_ref[COTANGENT : COTANGENT + TOKENS, sl]
        d_near = expand(w_ref[DSCORES : DSCORES + 64, sl])
        p_near = expand(w_ref[PROBS : PROBS + 64, sl])
        d_far = w_ref[DSCORES + 64 : DSCORES + KEYS, sl]
        p_far = w_ref[PROBS + 64 : PROBS + KEYS, sl]
        dq = mm(d_near, loc_ref[0:LOCAL, sl], ((0,), (0,))) + mm(d_far, w_ref[0:REMOTE, sl], ((0,), (0,)))
        dq_ref[:, sl] = (dq * SCALE).astype(BF16)
        dk = mm(d_near, q) * SCALE
        dv = mm(p_near, c)
        gk_ref[:, sl] = dk[0:128] + mm(spread, dk[128:224].astype(BF16))
        gv_ref[:, sl] = dv[0:128] + mm(spread, dv[128:224].astype(BF16))
        dk = mm(d_far, q) * SCALE
        dv = mm(p_far, c)
        g3_ref[0:16, sl] = dk[0:16].astype(BF16)
        g3_ref[16:32, sl] = dv[0:16].astype(BF16)
        g4a_ref[:, sl] = jnp.concatenate([dk[16:24], dv[16:24]], axis=0).astype(BF16)
        g4b_ref[:, sl] = jnp.concatenate([dk[24:32], dv[24:32]], axis=0).astype(BF16)
        gf_ref[0:FAR, sl] = dk[32:80].astype(BF16)
        gf_ref[FAR : 2 * FAR, sl] = dv[32:80].astype(BF16)
    row, col = iota2(PEERS * 8, 2 * FAR)
    is_key = col < FAR
    place = far_column(me, jnp.where(is_key, col, col - FAR)) + jnp.where(is_key, 0, 4)
    slot_ref[:, 0:WIDTH] = mm(mat(row == place, 1.0), gf_ref[...]).astype(BF16)
    slot_ref[:, WIDTH:] = jnp.zeros((PEERS * 8, 128), BF16)


def slope_kernel(s_ref, slot_in, slot_out, tile_ref, sem):
    value = jnp.sum(jnp.sum(s_ref[...], axis=0), axis=1, keepdims=True)
    high, middle, low = three_parts(value)
    lane = lax.broadcasted_iota(jnp.int32, (HEADS, 128), 1)
    tile = jnp.where(
        lane == 0, high, jnp.where(lane == 1, middle, jnp.where(lane == 2, low, 0.0))
    )
    tile_ref[...] = jnp.concatenate([tile] * PEERS, axis=0).astype(BF16)
    put = pltpu.make_async_copy(tile_ref, slot_out.at[:, pl.ds(WIDTH, 128)], sem)
    put.start()
    put.wait()


def final_kernel(gk_ref, gv_ref, r3_ref, r4a_ref, r4b_ref, r_ref, ok_ref, ov_ref, os_ref):
    me = lax.axis_index("seq")
    row, col = iota2(TOKENS, PEERS * 8)
    apart = (col >> 3) ^ me
    line = col & 7
    shift = jnp.where(apart >= 16, 7, jnp.where(apart >= 8, 6, 5))
    weight = jnp.where(
        apart >= 16, 2.0**-7, jnp.where(apart >= 8, 2.0**-6, jnp.where(apart >= 4, 2.0**-5, 0.0))
    )
    covers = lax.shift_right_logical(row, shift)
    row3, col3 = iota2(TOKENS, 32)
    row4, col4 = iota2(TOKENS, 16)
    for out_ref, own_ref, which in ((ok_ref, gk_ref, 0), (ov_ref, gv_ref, 1)):
        total = own_ref[...]
        total += mm(mat(covers + 4 * which == line, weight), r_ref[:, 0:WIDTH])
        total += mm(mat((row3 >> 3) + 16 * which == col3, 2.0**-3), r3_ref[...])
        both = mat((row4 >> 4) + 8 * which == col4, 2.0**-4)
        total += mm(both, r4a_ref[...]) + mm(both, r4b_ref[...])
        out_ref[...] = total.astype(BF16)
    slopes = r_ref[:, WIDTH:].astype(F32).reshape(PEERS, HEADS, 128)
    value = jnp.sum(jnp.sum(slopes, axis=0), axis=1, keepdims=True)
    srow, scol = iota2(HEADS, 128)
    line = jnp.sum(jnp.where(srow == scol, value, 0.0), axis=0, keepdims=True)
    os_ref[...] = line[:, 0:HEADS]


def call(kernel, outs, ins, places=None, out_places=None, scratch=(), cost=1 << 20, alias=None, vmem=12):
    places = places or [pltpu.VMEM] * len(ins)
    out_places = out_places or [pltpu.VMEM] * len(outs)
    return pl.pallas_call(
        kernel,
        out_shape=[jax.ShapeDtypeStruct(s, t) for s, t in outs],
        in_specs=[pl.BlockSpec(memory_space=place) for place in places],
        out_specs=[pl.BlockSpec(memory_space=place) for place in out_places],
        scratch_shapes=list(scratch),
        input_output_aliases=alias or {},
        compiler_params=pltpu.CompilerParams(vmem_limit_bytes=vmem * 1024 * 1024),
        cost_estimate=pl.CostEstimate(flops=0, bytes_accessed=cost, transcendentals=0),
    )(*ins)


def swap(block, apart):
    return lax.ppermute(block, "seq", [(i, i ^ apart) for i in range(PEERS)])


def exchange(slots):
    width = slots.shape[-1]
    back = lax.all_to_all(slots.reshape(PEERS, 8, width), "seq", 0, 0)
    return back.reshape(PEERS * 8, width)


def per_device(queries, keys_in, values_in, cotangent, level_slope):
    q, k, v, c = queries[0], keys_in[0], values_in[0], cotangent[0]
    wide = WIDTH
    block = pltpu.VMEM((TOKENS, wide), BF16)
    low, l3, l4, slots = call(
        pool_kernel,
        [((STEP + 16, wide), BF16), ((32, wide), BF16), ((16, wide), BF16), ((PEERS, 8, wide), BF16)],
        (k, v, level_slope),
        [pl.ANY] * 3,
        scratch=[block, block, pltpu.SMEM((HEADS,), F32), pltpu.SemaphoreType.DMA((3,))],
        vmem=58,
    )
    far = exchange(slots)
    near3 = swap(l3, 1)
    near4a = swap(l4, 2)
    near4b = swap(l4, 3)
    loc, near = call(
        local_kernel,
        [((STEPS + 16, wide), BF16), ((128, wide), F32)],
        (q, c, k, v, low),
        [pl.ANY] * 4 + [pltpu.VMEM],
        scratch=[pltpu.VMEM((LOCAL, wide), BF16), pltpu.SemaphoreType.DMA((4,))],
        cost=LONG,
    )
    groups = lax.axis_size("dp")
    work, slopes = call(
        score_kernel,
        [((DSCORES + KEYS, wide), BF16), ((groups, HEADS, 128), F32)],
        (loc, near, near3, near4a, near4b, far),
    )
    slopes = lax.all_to_all(slopes, "dp", 0, 0)
    dq, gk, gv, g3, g4a, g4b, slots = call(
        grad_kernel,
        [((TOKENS, wide), BF16), ((TOKENS, wide), F32), ((TOKENS, wide), F32), ((32, wide), BF16),
         ((16, wide), BF16), ((16, wide), BF16), ((PEERS * 8, wide + 128), BF16)],
        (loc, work),
        scratch=[pltpu.VMEM((2 * FAR, wide), BF16)],
    )
    (slots,) = call(
        slope_kernel,
        [((PEERS * 8, wide + 128), BF16)],
        (slopes, slots),
        [pltpu.VMEM, pl.ANY],
        [pl.ANY],
        [pltpu.VMEM((PEERS * 8, 128), BF16), pltpu.SemaphoreType.DMA(())],
        alias={1: 0},
    )
    far = exchange(slots)
    near3 = swap(g3, 1)
    near4a = swap(g4a, 2)
    near4b = swap(g4b, 3)
    dk, dv, ds = call(
        final_kernel,
        [((TOKENS, wide), BF16), ((TOKENS, wide), BF16), ((1, HEADS), F32)],
        (gk, gv, near3, near4a, near4b, far),
    )
    return dq[None], dk[None], dv[None], ds.reshape(HEADS)


def solution(mesh):
    row = P("dp", "seq", None)
    return jax.shard_map(
        per_device,
        mesh=mesh,
        in_specs=(row, row, row, row, P()),
        out_specs=(row, row, row, P()),
        check_vma=False,
    )
```

```python
import math

import jax
import jax.numpy as jnp
from jax import lax
from jax.experimental import pallas as pl
from jax.experimental.pallas import tpu as pltpu
from jax.sharding import PartitionSpec as P

LOG_TWO = math.log(2.0)
HEADS = 8
HEAD_DIM = 128
WIDTH = HEADS * HEAD_DIM
TOKENS = 128
PEERS = 32
LEVELS = 8
KEYS = 144
FAR = 48
SCALE = 1.0 / math.sqrt(HEAD_DIM)
LONG = 1 << 28
F32 = jnp.float32
BF16 = jnp.bfloat16


def iota2(rows, cols):
    row = lax.broadcasted_iota(jnp.int32, (rows, cols), 0)
    col = lax.broadcasted_iota(jnp.int32, (rows, cols), 1)
    return row, col


def mat(mask, weight):
    return jnp.where(mask, weight, 0.0).astype(BF16)


def mm(left, right, dims=((1,), (0,))):
    return lax.dot_general(left, right, (dims, ((), ())), preferred_element_type=F32)


def pooling(rows, cols):
    row, col = iota2(rows, cols)
    return mat((col >> 1) == row, 0.5)


def three_parts(value):
    high = value.astype(BF16).astype(F32)
    rest = value - high
    middle = rest.astype(BF16).astype(F32)
    return high, middle, rest - middle


LOCAL = 224
COARSE = 96
STEP = 2 * COARSE
REMOTE = 80
PROBS = 2 * REMOTE
DSCORES = PROBS + KEYS
QUERY = LOCAL
COTANGENT = LOCAL + TOKENS
STEPS = LOCAL + 2 * TOKENS


def pool_kernel(
    k_hbm, v_hbm, slope_hbm, low_ref, l3_ref, l4_ref, slot_ref, k_ref, v_ref, slope_ref, sems
):
    me = lax.axis_index("seq")
    fetch_k = pltpu.make_async_copy(k_hbm, k_ref, sems.at[0])
    fetch_v = pltpu.make_async_copy(v_hbm, v_ref, sems.at[1])
    fetch_slope = pltpu.make_async_copy(slope_hbm, slope_ref, sems.at[2])
    fetch_k.start()
    fetch_v.start()
    fetch_slope.start()
    half = pooling(64, 128)
    quarter = pooling(32, 64)
    fetch_slope.wait()
    line = lax.broadcasted_iota(jnp.int32, (16, HEAD_DIM), 0)
    for h in range(HEADS):
        high, middle, low = three_parts(jnp.full((16, HEAD_DIM), LOG_TWO + slope_ref[h], F32))
        part = jnp.where(line == 0, high, jnp.where(line == 1, middle, jnp.where(line == 2, low, 0.0)))
        low_ref[STEP : STEP + 16, h * HEAD_DIM : (h + 1) * HEAD_DIM] = part.astype(BF16)
    l2 = []
    for fetch, held, at in ((fetch_k, k_ref, 0), (fetch_v, v_ref, COARSE)):
        fetch.wait()
        one = mm(half, held[...]).astype(BF16)
        low_ref[at : at + 64, :] = one
        two = mm(quarter, one).astype(BF16)
        low_ref[at + 64 : at + 96, :] = two
        l2.append(two)
    l3 = mm(quarter, jnp.concatenate(l2, axis=0)).astype(BF16)
    l3_ref[...] = l3
    l4 = mm(pooling(16, 32), l3).astype(BF16)
    l4_ref[...] = l4
    row, col = iota2(16, 16)
    l5 = mm(pooling(16, 16), l4).astype(BF16)
    m6 = mat((row < 8) & ((row & 3) < 2) & ((col >> 1) == ((row >> 2) * 2 + (row & 3))), 0.5)
    l6 = mm(m6, l5).astype(BF16)
    m7 = mat((row < 8) & ((row & 3) == 0) & ((col >> 1) == (row >> 1)), 0.5)
    l7 = mm(m7, l6).astype(BF16)
    b5, b6, b7 = l5[0:8], l6[0:8], l7[0:8]
    base7 = ((me >> 4) ^ 1) << 4
    base6 = ((me >> 3) ^ 1) << 3
    base5 = ((me >> 2) ^ 1) << 2
    base4 = (me >> 2) << 2
    for i in range(16):
        slot_ref[base7 + i] = b7
    for i in range(8):
        slot_ref[base6 + i] = b6
    for i in range(4):
        slot_ref[base5 + i] = b5
    for i in range(4):
        slot_ref[base4 + i] = jnp.zeros((8, WIDTH), BF16)


def far_column(me, line):
    at5 = ((((me >> 2) ^ 1) << 2) + (line >> 2)) * 8 + (line & 3)
    six = line - 16
    at6 = ((((me >> 3) ^ 1) << 3) + (six >> 1)) * 8 + (six & 1)
    at7 = ((((me >> 4) ^ 1) << 4) + (line - 32)) * 8
    return jnp.where(line < 16, at5, jnp.where(line < 32, at6, at7))


def local_kernel(q_hbm, c_hbm, k_hbm, v_hbm, low_ref, loc_ref, s_ref, v_ref, sems):
    moves = (
        (k_hbm, loc_ref.at[pl.ds(0, TOKENS)]),
        (q_hbm, loc_ref.at[pl.ds(QUERY, TOKENS)]),
        (v_hbm, v_ref.at[pl.ds(0, TOKENS)]),
        (c_hbm, loc_ref.at[pl.ds(COTANGENT, TOKENS)]),
    )
    fetches = [pltpu.make_async_copy(a, b, sems.at[i]) for i, (a, b) in enumerate(moves)]
    for fetch in fetches:
        fetch.start()
    loc_ref[TOKENS:LOCAL, :] = low_ref[0:COARSE, :]
    v_ref[TOKENS:LOCAL, :] = low_ref[COARSE : 2 * COARSE, :]
    loc_ref[STEPS : STEPS + 16, :] = low_ref[STEP : STEP + 16, :]
    lane = lax.broadcasted_iota(jnp.int32, (1, TOKENS), 1)
    quarter = lane >> 5
    lower = lane < 64


    def compact(full):
        def by_quarter(blocks):
            return jnp.where(
                quarter < 2,
                jnp.where(quarter == 0, blocks[0], blocks[1]),
                jnp.where(quarter == 2, blocks[2], blocks[3]),
            )

        zero = by_quarter([full[32 * g : 32 * g + 32] for g in range(4)])
        one = by_quarter([full[128 + 16 * (g ^ 1) : 144 + 16 * (g ^ 1)] for g in range(4)])
        two = jnp.where(lower, full[208:224], full[192:208])
        return zero, one, two

    step_all = jnp.sum(low_ref[STEP : STEP + 16, :].astype(F32), axis=0, keepdims=True)
    for which, (held, at) in enumerate(((loc_ref, QUERY), (v_ref, COTANGENT))):
        fetches[2 * which].wait()
        fetches[2 * which + 1].wait()
        for h in range(HEADS):
            sl = slice(h * HEAD_DIM, (h + 1) * HEAD_DIM)
            raw = mm(held[0:LOCAL, sl], loc_ref[at : at + TOKENS, sl], ((1,), (1,)))
            zero, one, two = compact(raw)
            if which == 0:
                step = step_all[:, sl]
                zero, one, two = zero * SCALE, one * SCALE + step, two * SCALE + 2 * step
            s_ref[64 * which : 64 * which + 64, sl] = jnp.concatenate([zero, one, two], axis=0)


def score_kernel(loc_ref, near_ref, r3_ref, r4a_ref, r4b_ref, r_ref, w_ref, s_ref):
    me = lax.axis_index("seq")
    row, col = iota2(FAR, PEERS * 8)
    place = far_column(me, row)
    far = r_ref[...]
    prow, pcol = iota2(16, 16)
    for which in range(2):
        at = REMOTE * which
        w_ref[at : at + 16, :] = r3_ref[16 * which : 16 * which + 16, :]
        first = mat((prow < 8) & (pcol == prow + 8 * which), 1.0)
        second = mat((prow >= 8) & (pcol == prow - 8 + 8 * which), 1.0)
        four = mm(first, r4a_ref[...]) + mm(second, r4b_ref[...])
        w_ref[at + 16 : at + 32, :] = four.astype(BF16)
        w_ref[at + 32 : at + 80, :] = mm(mat(col == place + 4 * which, 1.0), far).astype(BF16)
    step_all = jnp.sum(loc_ref[STEPS : STEPS + 16, :].astype(F32), axis=0, keepdims=True)
    total = [None] * HEADS
    for h in range(HEADS):
        sl = slice(h * HEAD_DIM, (h + 1) * HEAD_DIM)
        raw = mm(w_ref[0:REMOTE, sl], loc_ref[QUERY : QUERY + TOKENS, sl], ((1,), (1,)))
        step = step_all[:, sl]
        parts = [near_ref[0:64, sl]]
        parts += [raw[16 * i : 16 * i + 16] * SCALE + (i + 3) * step for i in range(5)]
        scores = jnp.concatenate(parts, axis=0)
        top = jnp.max(scores, axis=0, keepdims=True)
        expo = jnp.exp(scores - top)
        probs = expo * (1.0 / jnp.sum(expo, axis=0, keepdims=True))
        probs_b = probs.astype(BF16)
        raw = mm(w_ref[REMOTE : 2 * REMOTE, sl], loc_ref[COTANGENT : COTANGENT + TOKENS, sl], ((1,), (1,)))
        dprobs = jnp.concatenate([near_ref[64:128, sl], raw], axis=0)
        delta = jnp.sum(probs_b.astype(F32) * dprobs, axis=0, keepdims=True)
        dscores = probs * (dprobs - delta)
        w_ref[PROBS : PROBS + KEYS, sl] = probs_b
        w_ref[DSCORES : DSCORES + KEYS, sl] = dscores.astype(BF16)
        acc = None
        for level in range(1, LEVELS):
            at = 16 + 16 * level
            term = level * (dscores[at : at + 8] + dscores[at + 8 : at + 16])
            acc = term if acc is None else acc + term
        total[h] = jnp.sum(acc, axis=0, keepdims=True)
    tile = jnp.concatenate(total, axis=0)
    for i in range(s_ref.shape[0]):
        s_ref[i] = tile


def far_grad_kernel(loc_ref, w_ref, g3_ref, g4a_ref, g4b_ref, gf_ref):
    for h in range(HEADS):
        sl = slice(h * HEAD_DIM, (h + 1) * HEAD_DIM)
        q, c = loc_ref[QUERY : QUERY + TOKENS, sl], loc_ref[COTANGENT : COTANGENT + TOKENS, sl]
        dk = mm(w_ref[DSCORES + 64 : DSCORES + KEYS, sl], q) * SCALE
        dv = mm(w_ref[PROBS + 64 : PROBS + KEYS, sl], c)
        g3_ref[0:16, sl] = dk[0:16].astype(BF16)
        g3_ref[16:32, sl] = dv[0:16].astype(BF16)
        g4a_ref[:, sl] = jnp.concatenate([dk[16:24], dv[16:24]], axis=0).astype(BF16)
        g4b_ref[:, sl] = jnp.concatenate([dk[24:32], dv[24:32]], axis=0).astype(BF16)
        gf_ref[0:FAR, sl] = dk[32:80].astype(BF16)
        gf_ref[FAR : 2 * FAR, sl] = dv[32:80].astype(BF16)


def grad_kernel(loc_ref, w_ref, gf_ref, dq_ref, gk_ref, gv_ref, slot_ref):
    me = lax.axis_index("seq")
    lane = lax.broadcasted_iota(jnp.int32, (1, TOKENS), 1)
    quarter = lane >> 5
    lower = lane < 64

    srow, scol = iota2(TOKENS, 96)
    spread = jnp.where(
        (scol < 64) & (scol == (srow >> 1)),
        0.5,
        jnp.where((scol >= 64) & (scol - 64 == (srow >> 2)), 0.25, 0.0),
    ).astype(BF16)

    def expand(part):
        part = part.astype(F32)
        zero, one, two = part[0:32], part[32:48], part[48:64]
        rows = [jnp.where(quarter == g, zero, 0.0) for g in range(4)]
        rows += [jnp.where(quarter == (g ^ 1), one, 0.0) for g in range(4)]
        rows += [jnp.where(lower, 0.0, two), jnp.where(lower, two, 0.0)]
        return jnp.concatenate(rows, axis=0).astype(BF16)

    for h in range(HEADS):
        sl = slice(h * HEAD_DIM, (h + 1) * HEAD_DIM)
        q, c = loc_ref[QUERY : QUERY + TOKENS, sl], loc_ref[COTANGENT : COTANGENT + TOKENS, sl]
        d_near = expand(w_ref[DSCORES : DSCORES + 64, sl])
        p_near = expand(w_ref[PROBS : PROBS + 64, sl])
        d_far = w_ref[DSCORES + 64 : DSCORES + KEYS, sl]
        dq = mm(d_near, loc_ref[0:LOCAL, sl], ((0,), (0,))) + mm(d_far, w_ref[0:REMOTE, sl], ((0,), (0,)))
        dq_ref[:, sl] = (dq * SCALE).astype(BF16)
        dk = mm(d_near, q) * SCALE
        dv = mm(p_near, c)
        gk_ref[:, sl] = dk[0:128] + mm(spread, dk[128:224].astype(BF16))
        gv_ref[:, sl] = dv[0:128] + mm(spread, dv[128:224].astype(BF16))
    row, col = iota2(PEERS * 8, 2 * FAR)
    is_key = col < FAR
    place = far_column(me, jnp.where(is_key, col, col - FAR)) + jnp.where(is_key, 0, 4)
    slot_ref[:, 0:WIDTH] = mm(mat(row == place, 1.0), gf_ref[...]).astype(BF16)
    slot_ref[:, WIDTH:] = jnp.zeros((PEERS * 8, 128), BF16)


def slope_kernel(s_ref, near_in, slot_in, slot_out, tile_ref, sem):
    value = jnp.sum(jnp.sum(s_ref[...], axis=0), axis=1, keepdims=True)
    high, middle, low = three_parts(value)
    lane = lax.broadcasted_iota(jnp.int32, (HEADS, 128), 1)
    tile = jnp.where(
        lane == 0, high, jnp.where(lane == 1, middle, jnp.where(lane == 2, low, 0.0))
    )
    tile_ref[...] = jnp.concatenate([tile] * PEERS, axis=0).astype(BF16)
    put = pltpu.make_async_copy(tile_ref, slot_out.at[:, pl.ds(WIDTH, 128)], sem)
    put.start()
    put.wait()


def final_kernel(gk_ref, gv_ref, r3_ref, r4a_ref, r4b_ref, r_ref, ok_ref, ov_ref, os_ref):
    me = lax.axis_index("seq")
    row, col = iota2(TOKENS, PEERS * 8)
    apart = (col >> 3) ^ me
    line = col & 7
    shift = jnp.where(apart >= 16, 7, jnp.where(apart >= 8, 6, 5))
    weight = jnp.where(
        apart >= 16, 2.0**-7, jnp.where(apart >= 8, 2.0**-6, jnp.where(apart >= 4, 2.0**-5, 0.0))
    )
    covers = lax.shift_right_logical(row, shift)
    row3, col3 = iota2(TOKENS, 32)
    row4, col4 = iota2(TOKENS, 16)
    for out_ref, own_ref, which in ((ok_ref, gk_ref, 0), (ov_ref, gv_ref, 1)):
        total = own_ref[...]
        total += mm(mat(covers + 4 * which == line, weight), r_ref[:, 0:WIDTH])
        total += mm(mat((row3 >> 3) + 16 * which == col3, 2.0**-3), r3_ref[...])
        both = mat((row4 >> 4) + 8 * which == col4, 2.0**-4)
        total += mm(both, r4a_ref[...]) + mm(both, r4b_ref[...])
        out_ref[...] = total.astype(BF16)
    slopes = r_ref[:, WIDTH:].astype(F32).reshape(PEERS, HEADS, 128)
    value = jnp.sum(jnp.sum(slopes, axis=0), axis=1, keepdims=True)
    srow, scol = iota2(HEADS, 128)
    line = jnp.sum(jnp.where(srow == scol, value, 0.0), axis=0, keepdims=True)
    os_ref[...] = line[:, 0:HEADS]


def call(kernel, outs, ins, places=None, out_places=None, scratch=(), cost=1 << 20, alias=None, vmem=12):
    places = places or [pltpu.VMEM] * len(ins)
    out_places = out_places or [pltpu.VMEM] * len(outs)
    return pl.pallas_call(
        kernel,
        out_shape=[jax.ShapeDtypeStruct(s, t) for s, t in outs],
        in_specs=[pl.BlockSpec(memory_space=place) for place in places],
        out_specs=[pl.BlockSpec(memory_space=place) for place in out_places],
        scratch_shapes=list(scratch),
        input_output_aliases=alias or {},
        compiler_params=pltpu.CompilerParams(vmem_limit_bytes=vmem * 1024 * 1024),
        cost_estimate=pl.CostEstimate(flops=0, bytes_accessed=cost, transcendentals=0),
    )(*ins)


def swap(block, apart):
    return lax.ppermute(block, "seq", [(i, i ^ apart) for i in range(PEERS)])


def exchange(slots):
    width = slots.shape[-1]
    back = lax.all_to_all(slots.reshape(PEERS, 8, width), "seq", 0, 0)
    return back.reshape(PEERS * 8, width)


def per_device(queries, keys_in, values_in, cotangent, level_slope):
    q, k, v, c = queries[0], keys_in[0], values_in[0], cotangent[0]
    wide = WIDTH
    block = pltpu.VMEM((TOKENS, wide), BF16)
    low, l3, l4, slots = call(
        pool_kernel,
        [((STEP + 16, wide), BF16), ((32, wide), BF16), ((16, wide), BF16), ((PEERS, 8, wide), BF16)],
        (k, v, level_slope),
        [pl.ANY] * 3,
        scratch=[block, block, pltpu.SMEM((HEADS,), F32), pltpu.SemaphoreType.DMA((3,))],
        vmem=58,
    )
    far = exchange(slots)
    near3 = swap(l3, 1)
    near4a = swap(l4, 2)
    near4b = swap(l4, 3)
    loc, near = call(
        local_kernel,
        [((STEPS + 16, wide), BF16), ((128, wide), F32)],
        (q, c, k, v, low),
        [pl.ANY] * 4 + [pltpu.VMEM],
        scratch=[pltpu.VMEM((LOCAL, wide), BF16), pltpu.SemaphoreType.DMA((4,))],
        cost=LONG,
    )
    groups = lax.axis_size("dp")
    work, slopes = call(
        score_kernel,
        [((DSCORES + KEYS, wide), BF16), ((groups, HEADS, 128), F32)],
        (loc, near, near3, near4a, near4b, far),
    )
    slopes = lax.all_to_all(slopes, "dp", 0, 0)
    g3, g4a, g4b, gf = call(
        far_grad_kernel,
        [((32, wide), BF16), ((16, wide), BF16), ((16, wide), BF16), ((2 * FAR, wide), BF16)],
        (loc, work),
    )
    near3 = swap(g3, 1)
    dq, gk, gv, slots = call(
        grad_kernel,
        [((TOKENS, wide), BF16), ((TOKENS, wide), F32), ((TOKENS, wide), F32),
         ((PEERS * 8, wide + 128), BF16)],
        (loc, work, gf),
        cost=LONG,
    )
    (slots,) = call(
        slope_kernel,
        [((PEERS * 8, wide + 128), BF16)],
        (slopes, near3, slots),
        [pltpu.VMEM, pl.ANY, pl.ANY],
        [pl.ANY],
        [pltpu.VMEM((PEERS * 8, 128), BF16), pltpu.SemaphoreType.DMA(())],
        alias={2: 0},
    )
    far = exchange(slots)
    near4a = swap(g4a, 2)
    near4b = swap(g4b, 3)
    dk, dv, ds = call(
        final_kernel,
        [((TOKENS, wide), BF16), ((TOKENS, wide), BF16), ((1, HEADS), F32)],
        (gk, gv, near3, near4a, near4b, far),
    )
    return dq[None], dk[None], dv[None], ds.reshape(HEADS)


def solution(mesh):
    row = P("dp", "seq", None)
    return jax.shard_map(
        per_device,
        mesh=mesh,
        in_specs=(row, row, row, row, P()),
        out_specs=(row, row, row, P()),
        check_vma=False,
    )
```

```python
import math

import jax
import jax.numpy as jnp
from jax import lax
from jax.experimental import pallas as pl
from jax.experimental.pallas import tpu as pltpu
from jax.sharding import PartitionSpec as P

LOG_TWO = math.log(2.0)
HEADS = 8
HEAD_DIM = 128
WIDTH = HEADS * HEAD_DIM
TOKENS = 128
PEERS = 32
LEVELS = 8
KEYS = 144
FAR = 48
SCALE = 1.0 / math.sqrt(HEAD_DIM)
LONG = 1 << 28
F32 = jnp.float32
BF16 = jnp.bfloat16


def iota2(rows, cols):
    row = lax.broadcasted_iota(jnp.int32, (rows, cols), 0)
    col = lax.broadcasted_iota(jnp.int32, (rows, cols), 1)
    return row, col


def mat(mask, weight):
    return jnp.where(mask, weight, 0.0).astype(BF16)


def mm(left, right, dims=((1,), (0,))):
    return lax.dot_general(left, right, (dims, ((), ())), preferred_element_type=F32)


def pooling(rows, cols):
    row, col = iota2(rows, cols)
    return mat((col >> 1) == row, 0.5)


def three_parts(value):
    high = value.astype(BF16).astype(F32)
    rest = value - high
    middle = rest.astype(BF16).astype(F32)
    return high, middle, rest - middle


LOCAL = 224
COARSE = 96
STEP = 2 * COARSE
REMOTE = 80
PROBS = 2 * REMOTE
DSCORES = PROBS + KEYS
HALF = WIDTH // 2
QUERY = LOCAL
COTANGENT = LOCAL + TOKENS
STEPS = LOCAL + 2 * TOKENS


def pool_kernel(
    k_hbm, v_hbm, slope_hbm, low_ref, l3_ref, l4_ref, slot_ref, k_ref, v_ref, slope_ref, sems
):
    me = lax.axis_index("seq")
    fetch_k = pltpu.make_async_copy(k_hbm, k_ref, sems.at[0])
    fetch_v = pltpu.make_async_copy(v_hbm, v_ref, sems.at[1])
    fetch_slope = pltpu.make_async_copy(slope_hbm, slope_ref, sems.at[2])
    fetch_k.start()
    fetch_v.start()
    fetch_slope.start()
    half = pooling(64, 128)
    quarter = pooling(32, 64)
    fetch_slope.wait()
    line = lax.broadcasted_iota(jnp.int32, (16, HEAD_DIM), 0)
    for h in range(HEADS):
        high, middle, low = three_parts(jnp.full((16, HEAD_DIM), LOG_TWO + slope_ref[h], F32))
        part = jnp.where(line == 0, high, jnp.where(line == 1, middle, jnp.where(line == 2, low, 0.0)))
        low_ref[STEP : STEP + 16, h * HEAD_DIM : (h + 1) * HEAD_DIM] = part.astype(BF16)
    l2 = []
    for fetch, held, at in ((fetch_k, k_ref, 0), (fetch_v, v_ref, COARSE)):
        fetch.wait()
        one = mm(half, held[...]).astype(BF16)
        low_ref[at : at + 64, :] = one
        two = mm(quarter, one).astype(BF16)
        low_ref[at + 64 : at + 96, :] = two
        l2.append(two)
    l3 = mm(quarter, jnp.concatenate(l2, axis=0)).astype(BF16)
    l3_ref[...] = l3
    l4 = mm(pooling(16, 32), l3).astype(BF16)
    l4_ref[...] = l4
    row, col = iota2(16, 16)
    l5 = mm(pooling(16, 16), l4).astype(BF16)
    m6 = mat((row < 8) & ((row & 3) < 2) & ((col >> 1) == ((row >> 2) * 2 + (row & 3))), 0.5)
    l6 = mm(m6, l5).astype(BF16)
    m7 = mat((row < 8) & ((row & 3) == 0) & ((col >> 1) == (row >> 1)), 0.5)
    l7 = mm(m7, l6).astype(BF16)
    b5, b6, b7 = l5[0:8], l6[0:8], l7[0:8]
    base7 = ((me >> 4) ^ 1) << 4
    base6 = ((me >> 3) ^ 1) << 3
    base5 = ((me >> 2) ^ 1) << 2
    base4 = (me >> 2) << 2
    for i in range(16):
        slot_ref[base7 + i] = b7
    for i in range(8):
        slot_ref[base6 + i] = b6
    for i in range(4):
        slot_ref[base5 + i] = b5
    for i in range(4):
        slot_ref[base4 + i] = jnp.zeros((8, WIDTH), BF16)


def far_column(me, line):
    at5 = ((((me >> 2) ^ 1) << 2) + (line >> 2)) * 8 + (line & 3)
    six = line - 16
    at6 = ((((me >> 3) ^ 1) << 3) + (six >> 1)) * 8 + (six & 1)
    at7 = ((((me >> 4) ^ 1) << 4) + (line - 32)) * 8
    return jnp.where(line < 16, at5, jnp.where(line < 32, at6, at7))


def local_kernel(q_hbm, c_hbm, k_hbm, v_hbm, low_ref, loc_ref, s_ref, v_ref, sems):
    moves = (
        (k_hbm, loc_ref.at[pl.ds(0, TOKENS)]),
        (q_hbm, loc_ref.at[pl.ds(QUERY, TOKENS)]),
        (v_hbm, v_ref.at[pl.ds(0, TOKENS)]),
        (c_hbm, loc_ref.at[pl.ds(COTANGENT, TOKENS)]),
    )
    fetches = [pltpu.make_async_copy(a, b, sems.at[i]) for i, (a, b) in enumerate(moves)]
    for fetch in fetches:
        fetch.start()
    loc_ref[TOKENS:LOCAL, :] = low_ref[0:COARSE, :]
    v_ref[TOKENS:LOCAL, :] = low_ref[COARSE : 2 * COARSE, :]
    loc_ref[STEPS : STEPS + 16, :] = low_ref[STEP : STEP + 16, :]
    lane = lax.broadcasted_iota(jnp.int32, (1, TOKENS), 1)
    quarter = lane >> 5
    lower = lane < 64


    def compact(full):
        def by_quarter(blocks):
            return jnp.where(
                quarter < 2,
                jnp.where(quarter == 0, blocks[0], blocks[1]),
                jnp.where(quarter == 2, blocks[2], blocks[3]),
            )

        zero = by_quarter([full[32 * g : 32 * g + 32] for g in range(4)])
        one = by_quarter([full[128 + 16 * (g ^ 1) : 144 + 16 * (g ^ 1)] for g in range(4)])
        two = jnp.where(lower, full[208:224], full[192:208])
        return zero, one, two

    step_all = jnp.sum(low_ref[STEP : STEP + 16, :].astype(F32), axis=0, keepdims=True)
    for which, (held, at) in enumerate(((loc_ref, QUERY), (v_ref, COTANGENT))):
        fetches[2 * which].wait()
        fetches[2 * which + 1].wait()
        for h in range(HEADS):
            sl = slice(h * HEAD_DIM, (h + 1) * HEAD_DIM)
            raw = mm(held[0:LOCAL, sl], loc_ref[at : at + TOKENS, sl], ((1,), (1,)))
            zero, one, two = compact(raw)
            if which == 0:
                step = step_all[:, sl]
                zero, one, two = zero * SCALE, one * SCALE + step, two * SCALE + 2 * step
            s_ref[64 * which : 64 * which + 64, sl] = jnp.concatenate([zero, one, two], axis=0)


def score_kernel(loc_ref, near_ref, r3_ref, r4a_ref, r4b_ref, r_ref, w_ref, s_ref):
    me = lax.axis_index("seq")
    row, col = iota2(FAR, PEERS * 8)
    place = far_column(me, row)
    far = r_ref[...]
    prow, pcol = iota2(16, 16)
    for which in range(2):
        at = REMOTE * which
        w_ref[at : at + 16, :] = r3_ref[16 * which : 16 * which + 16, :]
        first = mat((prow < 8) & (pcol == prow + 8 * which), 1.0)
        second = mat((prow >= 8) & (pcol == prow - 8 + 8 * which), 1.0)
        four = mm(first, r4a_ref[...]) + mm(second, r4b_ref[...])
        w_ref[at + 16 : at + 32, :] = four.astype(BF16)
        w_ref[at + 32 : at + 80, :] = mm(mat(col == place + 4 * which, 1.0), far).astype(BF16)
    step_all = jnp.sum(loc_ref[STEPS : STEPS + 16, :].astype(F32), axis=0, keepdims=True)
    total = [None] * HEADS
    for h in range(HEADS):
        sl = slice(h * HEAD_DIM, (h + 1) * HEAD_DIM)
        raw = mm(w_ref[0:REMOTE, sl], loc_ref[QUERY : QUERY + TOKENS, sl], ((1,), (1,)))
        step = step_all[:, sl]
        parts = [near_ref[0:64, sl]]
        parts += [raw[16 * i : 16 * i + 16] * SCALE + (i + 3) * step for i in range(5)]
        scores = jnp.concatenate(parts, axis=0)
        top = jnp.max(scores, axis=0, keepdims=True)
        expo = jnp.exp(scores - top)
        probs = expo * (1.0 / jnp.sum(expo, axis=0, keepdims=True))
        probs_b = probs.astype(BF16)
        raw = mm(w_ref[REMOTE : 2 * REMOTE, sl], loc_ref[COTANGENT : COTANGENT + TOKENS, sl], ((1,), (1,)))
        dprobs = jnp.concatenate([near_ref[64:128, sl], raw], axis=0)
        delta = jnp.sum(probs_b.astype(F32) * dprobs, axis=0, keepdims=True)
        dscores = probs * (dprobs - delta)
        w_ref[PROBS : PROBS + KEYS, sl] = probs_b
        w_ref[DSCORES : DSCORES + KEYS, sl] = dscores.astype(BF16)
        acc = None
        for level in range(1, LEVELS):
            at = 16 + 16 * level
            term = level * (dscores[at : at + 8] + dscores[at + 8 : at + 16])
            acc = term if acc is None else acc + term
        total[h] = jnp.sum(acc, axis=0, keepdims=True)
    tile = jnp.concatenate(total, axis=0)
    for i in range(s_ref.shape[0]):
        s_ref[i] = tile


def far_grad_kernel(loc_ref, w_ref, g3_ref, g4a_ref, g4b_ref, g5_ref, gf_ref):
    for h in range(HEADS):
        sl = slice(h * HEAD_DIM, (h + 1) * HEAD_DIM)
        q, c = loc_ref[QUERY : QUERY + TOKENS, sl], loc_ref[COTANGENT : COTANGENT + TOKENS, sl]
        dk = mm(w_ref[DSCORES + 64 : DSCORES + KEYS, sl], q) * SCALE
        dv = mm(w_ref[PROBS + 64 : PROBS + KEYS, sl], c)
        g3_ref[0:16, sl] = dk[0:16].astype(BF16)
        g3_ref[16:32, sl] = dv[0:16].astype(BF16)
        g4a_ref[:, sl] = jnp.concatenate([dk[16:24], dv[16:24]], axis=0).astype(BF16)
        g4b_ref[:, sl] = jnp.concatenate([dk[24:32], dv[24:32]], axis=0).astype(BF16)
        g5_ref[0:16, sl] = dk[32:48].astype(BF16)
        g5_ref[16:32, sl] = dv[32:48].astype(BF16)
        gf_ref[0:32, sl] = dk[48:80].astype(BF16)
        gf_ref[32:64, sl] = dv[48:80].astype(BF16)


def grad_kernel(loc_ref, w_ref, gf_ref, dq_ref, gk_ref, gv_ref, slot_ref):
    me = lax.axis_index("seq")
    lane = lax.broadcasted_iota(jnp.int32, (1, TOKENS), 1)
    quarter = lane >> 5
    lower = lane < 64

    srow, scol = iota2(TOKENS, 96)
    spread = jnp.where(
        (scol < 64) & (scol == (srow >> 1)),
        0.5,
        jnp.where((scol >= 64) & (scol - 64 == (srow >> 2)), 0.25, 0.0),
    ).astype(BF16)

    def expand(part):
        part = part.astype(F32)
        zero, one, two = part[0:32], part[32:48], part[48:64]
        rows = [jnp.where(quarter == g, zero, 0.0) for g in range(4)]
        rows += [jnp.where(quarter == (g ^ 1), one, 0.0) for g in range(4)]
        rows += [jnp.where(lower, 0.0, two), jnp.where(lower, two, 0.0)]
        return jnp.concatenate(rows, axis=0).astype(BF16)

    for h in range(HEADS):
        sl = slice(h * HEAD_DIM, (h + 1) * HEAD_DIM)
        q, c = loc_ref[QUERY : QUERY + TOKENS, sl], loc_ref[COTANGENT : COTANGENT + TOKENS, sl]
        d_near = expand(w_ref[DSCORES : DSCORES + 64, sl])
        p_near = expand(w_ref[PROBS : PROBS + 64, sl])
        d_far = w_ref[DSCORES + 64 : DSCORES + KEYS, sl]
        dq = mm(d_near, loc_ref[0:LOCAL, sl], ((0,), (0,))) + mm(d_far, w_ref[0:REMOTE, sl], ((0,), (0,)))
        dq_ref[:, sl] = (dq * SCALE).astype(BF16)
        dk = mm(d_near, q) * SCALE
        dv = mm(p_near, c)
        gk_ref[:, sl] = dk[0:128] + mm(spread, dk[128:224].astype(BF16))
        gv_ref[:, sl] = dv[0:128] + mm(spread, dv[128:224].astype(BF16))
    row, col = iota2(PEERS * 8, 64)
    is_key = col < 32
    line = jnp.where(is_key, col, col - 32) + 16
    place = far_column(me, line) + jnp.where(is_key, 0, 2)
    first = mm(mat(row == place, 1.0), gf_ref[:, 0:HALF])
    second = mm(mat(row == place + 4, 1.0), gf_ref[:, HALF:WIDTH])
    slot_ref[:, 0:HALF] = (first + second).astype(BF16)
    slot_ref[:, HALF:] = jnp.zeros((PEERS * 8, 128), BF16)


def slope_kernel(
    s_ref, r5_ref, g3_ref, g4a_ref, g4b_ref, slot_in, pair_ref, a_ref, b_ref, slot_out, tile_ref, sem
):
    me = lax.axis_index("seq")
    value = jnp.sum(jnp.sum(s_ref[...], axis=0), axis=1, keepdims=True)
    high, middle, low = three_parts(value)
    lane = lax.broadcasted_iota(jnp.int32, (HEADS, 128), 1)
    tile = jnp.where(
        lane == 0, high, jnp.where(lane == 1, middle, jnp.where(lane == 2, low, 0.0))
    )
    tile_ref[...] = jnp.concatenate([tile] * PEERS, axis=0).astype(BF16)
    put = pltpu.make_async_copy(tile_ref, slot_out.at[:, pl.ds(HALF, 128)], sem)
    put.start()
    row, col = iota2(16, 32)
    for apart, own_ref, out_ref in ((1, g3_ref, pair_ref), (2, g4a_ref, a_ref), (3, g4b_ref, b_ref)):
        size = own_ref.shape[0]
        out_ref[0:size, :] = own_ref[...]
        at = ((me & 3) ^ apart) * 4
        pick = ((row < 4) & (col == at + row)) | ((row >= 4) & (row < 8) & (col == at + row + 12))
        out_ref[size : size + 16, :] = mm(mat(pick, 1.0), r5_ref[...]).astype(BF16)
    put.wait()


def final_kernel(
    gk_ref, gv_ref, pair_ref, a_ref, b_ref, r5_ref, r_ref, ok_ref, ov_ref, os_ref
):
    me = lax.axis_index("seq")
    row, col = iota2(TOKENS, PEERS * 8)
    apart = (col >> 3) ^ me
    line = col & 7
    shift = jnp.where(apart >= 16, 7, 6)
    weight = jnp.where(apart >= 16, 2.0**-7, jnp.where(apart >= 8, 2.0**-6, 0.0))
    covers = lax.shift_right_logical(row, shift)
    row3, col3 = iota2(TOKENS, 48)
    row4, col4 = iota2(TOKENS, 32)
    for out_ref, own_ref, which in ((ok_ref, gk_ref, 0), (ov_ref, gv_ref, 1)):
        near = own_ref[...]
        three = jnp.where((row3 >> 3) + 16 * which == col3, 2.0**-3, 0.0)
        five = jnp.where((row3 >> 5) + 32 + 4 * which == col3, 2.0**-5, 0.0)
        near += mm((three + five).astype(BF16), pair_ref[...])
        four = jnp.where((row4 >> 4) + 8 * which == col4, 2.0**-4, 0.0)
        five = jnp.where((row4 >> 5) + 16 + 4 * which == col4, 2.0**-5, 0.0)
        both = (four + five).astype(BF16)
        near += mm(both, a_ref[...]) + mm(both, b_ref[...])
        mine = mat((row4 >> 5) + 4 * (me & 3) + 16 * which == col4, 2.0**-5)
        near += mm(mine, r5_ref[...])
        for half in range(2):
            sl = slice(HALF * half, HALF * half + HALF)
            far = mat(covers + 2 * which + 4 * half == line, weight)
            out_ref[:, sl] = (near[:, sl] + mm(far, r_ref[:, 0:HALF])).astype(BF16)
    slopes = r_ref[:, HALF:].astype(F32).reshape(PEERS, HEADS, 128)
    value = jnp.sum(jnp.sum(slopes, axis=0), axis=1, keepdims=True)
    srow, scol = iota2(HEADS, 128)
    line = jnp.sum(jnp.where(srow == scol, value, 0.0), axis=0, keepdims=True)
    os_ref[...] = line[:, 0:HEADS]


def call(kernel, outs, ins, places=None, out_places=None, scratch=(), cost=1 << 20, alias=None, vmem=12):
    places = places or [pltpu.VMEM] * len(ins)
    out_places = out_places or [pltpu.VMEM] * len(outs)
    return pl.pallas_call(
        kernel,
        out_shape=[jax.ShapeDtypeStruct(s, t) for s, t in outs],
        in_specs=[pl.BlockSpec(memory_space=place) for place in places],
        out_specs=[pl.BlockSpec(memory_space=place) for place in out_places],
        scratch_shapes=list(scratch),
        input_output_aliases=alias or {},
        compiler_params=pltpu.CompilerParams(vmem_limit_bytes=vmem * 1024 * 1024),
        cost_estimate=pl.CostEstimate(flops=0, bytes_accessed=cost, transcendentals=0),
    )(*ins)


def swap(block, apart):
    return lax.ppermute(block, "seq", [(i, i ^ apart) for i in range(PEERS)])


def exchange(slots):
    width = slots.shape[-1]
    back = lax.all_to_all(slots.reshape(PEERS, 8, width), "seq", 0, 0)
    return back.reshape(PEERS * 8, width)


def per_device(queries, keys_in, values_in, cotangent, level_slope):
    q, k, v, c = queries[0], keys_in[0], values_in[0], cotangent[0]
    wide = WIDTH
    block = pltpu.VMEM((TOKENS, wide), BF16)
    low, l3, l4, slots = call(
        pool_kernel,
        [((STEP + 16, wide), BF16), ((32, wide), BF16), ((16, wide), BF16), ((PEERS, 8, wide), BF16)],
        (k, v, level_slope),
        [pl.ANY] * 3,
        scratch=[block, block, pltpu.SMEM((HEADS,), F32), pltpu.SemaphoreType.DMA((3,))],
        vmem=58,
    )
    far = exchange(slots)
    near3 = swap(l3, 1)
    near4a = swap(l4, 2)
    near4b = swap(l4, 3)
    loc, near = call(
        local_kernel,
        [((STEPS + 16, wide), BF16), ((128, wide), F32)],
        (q, c, k, v, low),
        [pl.ANY] * 4 + [pltpu.VMEM],
        scratch=[pltpu.VMEM((LOCAL, wide), BF16), pltpu.SemaphoreType.DMA((4,))],
        cost=LONG,
    )
    groups = lax.axis_size("dp")
    work, slopes = call(
        score_kernel,
        [((DSCORES + KEYS, wide), BF16), ((groups, HEADS, 128), F32)],
        (loc, near, near3, near4a, near4b, far),
    )
    slopes = lax.all_to_all(slopes, "dp", 0, 0)
    g3, g4a, g4b, g5, gf = call(
        far_grad_kernel,
        [((32, wide), BF16), ((16, wide), BF16), ((16, wide), BF16), ((32, wide), BF16), ((64, wide), BF16)],
        (loc, work),
    )
    near5 = swap(g5, 4)
    dq, gk, gv, slots = call(
        grad_kernel,
        [((TOKENS, wide), BF16), ((TOKENS, wide), F32), ((TOKENS, wide), F32),
         ((PEERS * 8, HALF + 128), BF16)],
        (loc, work, gf),
        cost=LONG,
    )
    pair, four_a, four_b, slots = call(
        slope_kernel,
        [((48, wide), BF16), ((32, wide), BF16), ((32, wide), BF16), ((PEERS * 8, HALF + 128), BF16)],
        (slopes, near5, g3, g4a, g4b, slots),
        [pltpu.VMEM] * 5 + [pl.ANY],
        [pltpu.VMEM] * 3 + [pl.ANY],
        [pltpu.VMEM((PEERS * 8, 128), BF16), pltpu.SemaphoreType.DMA(())],
        alias={5: 3},
    )
    far = exchange(slots)
    pair = swap(pair, 1)
    four_a = swap(four_a, 2)
    four_b = swap(four_b, 3)
    dk, dv, ds = call(
        final_kernel,
        [((TOKENS, wide), BF16), ((TOKENS, wide), BF16), ((1, HEADS), F32)],
        (gk, gv, pair, four_a, four_b, near5, far),
    )
    return dq[None], dk[None], dv[None], ds.reshape(HEADS)


def solution(mesh):
    row = P("dp", "seq", None)
    return jax.shard_map(
        per_device,
        mesh=mesh,
        in_specs=(row, row, row, row, P()),
        out_specs=(row, row, row, P()),
        check_vma=False,
    )
```

```python
import math

import jax
import jax.numpy as jnp
from jax import lax
from jax.experimental import pallas as pl
from jax.experimental.pallas import tpu as pltpu
from jax.sharding import PartitionSpec as P

LOG_TWO = math.log(2.0)
HEADS = 8
HEAD_DIM = 128
WIDTH = HEADS * HEAD_DIM
TOKENS = 128
PEERS = 32
LEVELS = 8
KEYS = 144
FAR = 48
SCALE = 1.0 / math.sqrt(HEAD_DIM)
LONG = 1 << 28
F32 = jnp.float32
BF16 = jnp.bfloat16


def iota2(rows, cols):
    row = lax.broadcasted_iota(jnp.int32, (rows, cols), 0)
    col = lax.broadcasted_iota(jnp.int32, (rows, cols), 1)
    return row, col


def mat(mask, weight):
    return jnp.where(mask, weight, 0.0).astype(BF16)


def mm(left, right, dims=((1,), (0,))):
    return lax.dot_general(left, right, (dims, ((), ())), preferred_element_type=F32)


def pooling(rows, cols):
    row, col = iota2(rows, cols)
    return mat((col >> 1) == row, 0.5)


def three_parts(value):
    high = value.astype(BF16).astype(F32)
    rest = value - high
    middle = rest.astype(BF16).astype(F32)
    return high, middle, rest - middle


LOCAL = 224
COARSE = 96
STEP = 2 * COARSE
REMOTE = 80
PROBS = 2 * REMOTE
DSCORES = PROBS + KEYS
HALF = WIDTH // 2
QUERY = LOCAL
COTANGENT = LOCAL + TOKENS
STEPS = LOCAL + 2 * TOKENS


def pool_kernel(
    k_hbm, v_hbm, slope_hbm, low_ref, l3_ref, l4_ref, slot_ref, k_ref, v_ref, slope_ref, sems
):
    me = lax.axis_index("seq")
    fetch_k = pltpu.make_async_copy(k_hbm, k_ref, sems.at[0])
    fetch_v = pltpu.make_async_copy(v_hbm, v_ref, sems.at[1])
    fetch_slope = pltpu.make_async_copy(slope_hbm, slope_ref, sems.at[2])
    fetch_k.start()
    fetch_v.start()
    fetch_slope.start()
    half = pooling(64, 128)
    quarter = pooling(32, 64)
    fetch_slope.wait()
    line = lax.broadcasted_iota(jnp.int32, (16, HEAD_DIM), 0)
    for h in range(HEADS):
        high, middle, low = three_parts(jnp.full((16, HEAD_DIM), LOG_TWO + slope_ref[h], F32))
        part = jnp.where(line == 0, high, jnp.where(line == 1, middle, jnp.where(line == 2, low, 0.0)))
        low_ref[STEP : STEP + 16, h * HEAD_DIM : (h + 1) * HEAD_DIM] = part.astype(BF16)
    l2 = []
    for fetch, held, at in ((fetch_k, k_ref, 0), (fetch_v, v_ref, COARSE)):
        fetch.wait()
        one = mm(half, held[...]).astype(BF16)
        low_ref[at : at + 64, :] = one
        two = mm(quarter, one).astype(BF16)
        low_ref[at + 64 : at + 96, :] = two
        l2.append(two)
    l3 = mm(quarter, jnp.concatenate(l2, axis=0)).astype(BF16)
    l3_ref[...] = l3
    l4 = mm(pooling(16, 32), l3).astype(BF16)
    l4_ref[...] = l4
    row, col = iota2(16, 16)
    l5 = mm(pooling(16, 16), l4).astype(BF16)
    m6 = mat((row < 8) & ((row & 3) < 2) & ((col >> 1) == ((row >> 2) * 2 + (row & 3))), 0.5)
    l6 = mm(m6, l5).astype(BF16)
    m7 = mat((row < 8) & ((row & 3) == 0) & ((col >> 1) == (row >> 1)), 0.5)
    l7 = mm(m7, l6).astype(BF16)
    b5, b6, b7 = l5[0:8], l6[0:8], l7[0:8]
    base7 = ((me >> 4) ^ 1) << 4
    base6 = ((me >> 3) ^ 1) << 3
    base5 = ((me >> 2) ^ 1) << 2
    base4 = (me >> 2) << 2
    for i in range(16):
        slot_ref[base7 + i] = b7
    for i in range(8):
        slot_ref[base6 + i] = b6
    for i in range(4):
        slot_ref[base5 + i] = b5
    for i in range(4):
        slot_ref[base4 + i] = jnp.zeros((8, WIDTH), BF16)


def far_column(me, line):
    at5 = ((((me >> 2) ^ 1) << 2) + (line >> 2)) * 8 + (line & 3)
    six = line - 16
    at6 = ((((me >> 3) ^ 1) << 3) + (six >> 1)) * 8 + (six & 1)
    at7 = ((((me >> 4) ^ 1) << 4) + (line - 32)) * 8
    return jnp.where(line < 16, at5, jnp.where(line < 32, at6, at7))


def local_kernel(q_hbm, c_hbm, k_hbm, v_hbm, low_ref, loc_ref, s_ref, v_ref, sems):
    moves = (
        (k_hbm, loc_ref.at[pl.ds(0, TOKENS)]),
        (q_hbm, loc_ref.at[pl.ds(QUERY, TOKENS)]),
        (v_hbm, v_ref.at[pl.ds(0, TOKENS)]),
        (c_hbm, loc_ref.at[pl.ds(COTANGENT, TOKENS)]),
    )
    fetches = [pltpu.make_async_copy(a, b, sems.at[i]) for i, (a, b) in enumerate(moves)]
    for fetch in fetches:
        fetch.start()
    loc_ref[TOKENS:LOCAL, :] = low_ref[0:COARSE, :]
    v_ref[TOKENS:LOCAL, :] = low_ref[COARSE : 2 * COARSE, :]
    loc_ref[STEPS : STEPS + 16, :] = low_ref[STEP : STEP + 16, :]
    lane = lax.broadcasted_iota(jnp.int32, (1, TOKENS), 1)
    quarter = lane >> 5
    lower = lane < 64


    def compact(full):
        def by_quarter(blocks):
            return jnp.where(
                quarter < 2,
                jnp.where(quarter == 0, blocks[0], blocks[1]),
                jnp.where(quarter == 2, blocks[2], blocks[3]),
            )

        zero = by_quarter([full[32 * g : 32 * g + 32] for g in range(4)])
        one = by_quarter([full[128 + 16 * (g ^ 1) : 144 + 16 * (g ^ 1)] for g in range(4)])
        two = jnp.where(lower, full[208:224], full[192:208])
        return zero, one, two

    step_all = jnp.sum(low_ref[STEP : STEP + 16, :].astype(F32), axis=0, keepdims=True)
    for which, (held, at) in enumerate(((loc_ref, QUERY), (v_ref, COTANGENT))):
        fetches[2 * which].wait()
        fetches[2 * which + 1].wait()
        for h in range(HEADS):
            sl = slice(h * HEAD_DIM, (h + 1) * HEAD_DIM)
            raw = mm(held[0:LOCAL, sl], loc_ref[at : at + TOKENS, sl], ((1,), (1,)))
            zero, one, two = compact(raw)
            if which == 0:
                step = step_all[:, sl]
                zero, one, two = zero * SCALE, one * SCALE + step, two * SCALE + 2 * step
            s_ref[64 * which : 64 * which + 64, sl] = jnp.concatenate([zero, one, two], axis=0)


def score_kernel(loc_ref, near_ref, r3_ref, r4a_ref, r4b_ref, r_ref, w_ref, s_ref):
    me = lax.axis_index("seq")
    row, col = iota2(FAR, PEERS * 8)
    place = far_column(me, row)
    far = r_ref[...]
    prow, pcol = iota2(16, 16)
    for which in range(2):
        at = REMOTE * which
        w_ref[at : at + 16, :] = r3_ref[16 * which : 16 * which + 16, :]
        first = mat((prow < 8) & (pcol == prow + 8 * which), 1.0)
        second = mat((prow >= 8) & (pcol == prow - 8 + 8 * which), 1.0)
        four = mm(first, r4a_ref[...]) + mm(second, r4b_ref[...])
        w_ref[at + 16 : at + 32, :] = four.astype(BF16)
        w_ref[at + 32 : at + 80, :] = mm(mat(col == place + 4 * which, 1.0), far).astype(BF16)
    step_all = jnp.sum(loc_ref[STEPS : STEPS + 16, :].astype(F32), axis=0, keepdims=True)
    total = [None] * HEADS
    for h in range(HEADS):
        sl = slice(h * HEAD_DIM, (h + 1) * HEAD_DIM)
        raw = mm(w_ref[0:REMOTE, sl], loc_ref[QUERY : QUERY + TOKENS, sl], ((1,), (1,)))
        step = step_all[:, sl]
        parts = [near_ref[0:64, sl]]
        parts += [raw[16 * i : 16 * i + 16] * SCALE + (i + 3) * step for i in range(5)]
        scores = jnp.concatenate(parts, axis=0)
        top = jnp.max(scores, axis=0, keepdims=True)
        expo = jnp.exp(scores - top)
        probs = expo * (1.0 / jnp.sum(expo, axis=0, keepdims=True))
        probs_b = probs.astype(BF16)
        raw = mm(w_ref[REMOTE : 2 * REMOTE, sl], loc_ref[COTANGENT : COTANGENT + TOKENS, sl], ((1,), (1,)))
        dprobs = jnp.concatenate([near_ref[64:128, sl], raw], axis=0)
        delta = jnp.sum(probs_b.astype(F32) * dprobs, axis=0, keepdims=True)
        dscores = probs * (dprobs - delta)
        w_ref[PROBS : PROBS + KEYS, sl] = probs_b
        w_ref[DSCORES : DSCORES + KEYS, sl] = dscores.astype(BF16)
        acc = None
        for level in range(1, LEVELS):
            at = 16 + 16 * level
            term = level * (dscores[at : at + 8] + dscores[at + 8 : at + 16])
            acc = term if acc is None else acc + term
        total[h] = jnp.sum(acc, axis=0, keepdims=True)
    tile = jnp.concatenate(total, axis=0)
    for i in range(s_ref.shape[0]):
        s_ref[i] = tile


def far_grad_kernel(loc_ref, w_ref, g3_ref, cross_ref, g5_ref, gf_ref):
    upper = ((lax.axis_index("seq") >> 1) & 1) == 1
    for h in range(HEADS):
        sl = slice(h * HEAD_DIM, (h + 1) * HEAD_DIM)
        q, c = loc_ref[QUERY : QUERY + TOKENS, sl], loc_ref[COTANGENT : COTANGENT + TOKENS, sl]
        dk = mm(w_ref[DSCORES + 64 : DSCORES + KEYS, sl], q) * SCALE
        dv = mm(w_ref[PROBS + 64 : PROBS + KEYS, sl], c)
        g3_ref[0:16, sl] = dk[0:16].astype(BF16)
        g3_ref[16:32, sl] = dv[0:16].astype(BF16)
        cross_ref[0:16, sl] = jnp.concatenate([dk[16:24], dv[16:24]], axis=0).astype(BF16)
        cross_ref[16:32, sl] = jnp.concatenate([dk[24:32], dv[24:32]], axis=0).astype(BF16)
        low = jnp.concatenate([dk[32:40], dv[32:40]], axis=0)
        high = jnp.concatenate([dk[40:48], dv[40:48]], axis=0)
        cross_ref[32:48, sl] = jnp.where(upper, low, high).astype(BF16)
        g5_ref[:, sl] = jnp.where(upper, high, low).astype(BF16)
        gf_ref[0:32, sl] = dk[48:80].astype(BF16)
        gf_ref[32:64, sl] = dv[48:80].astype(BF16)


def grad_kernel(loc_ref, w_ref, gf_ref, dq_ref, gk_ref, gv_ref, slot_ref):
    me = lax.axis_index("seq")
    lane = lax.broadcasted_iota(jnp.int32, (1, TOKENS), 1)
    quarter = lane >> 5
    lower = lane < 64

    srow, scol = iota2(TOKENS, 96)
    spread = jnp.where(
        (scol < 64) & (scol == (srow >> 1)),
        0.5,
        jnp.where((scol >= 64) & (scol - 64 == (srow >> 2)), 0.25, 0.0),
    ).astype(BF16)

    def expand(part):
        part = part.astype(F32)
        zero, one, two = part[0:32], part[32:48], part[48:64]
        rows = [jnp.where(quarter == g, zero, 0.0) for g in range(4)]
        rows += [jnp.where(quarter == (g ^ 1), one, 0.0) for g in range(4)]
        rows += [jnp.where(lower, 0.0, two), jnp.where(lower, two, 0.0)]
        return jnp.concatenate(rows, axis=0).astype(BF16)

    for h in range(HEADS):
        sl = slice(h * HEAD_DIM, (h + 1) * HEAD_DIM)
        q, c = loc_ref[QUERY : QUERY + TOKENS, sl], loc_ref[COTANGENT : COTANGENT + TOKENS, sl]
        d_near = expand(w_ref[DSCORES : DSCORES + 64, sl])
        p_near = expand(w_ref[PROBS : PROBS + 64, sl])
        d_far = w_ref[DSCORES + 64 : DSCORES + KEYS, sl]
        dq = mm(d_near, loc_ref[0:LOCAL, sl], ((0,), (0,))) + mm(d_far, w_ref[0:REMOTE, sl], ((0,), (0,)))
        dq_ref[:, sl] = (dq * SCALE).astype(BF16)
        dk = mm(d_near, q) * SCALE
        dv = mm(p_near, c)
        gk_ref[:, sl] = dk[0:128] + mm(spread, dk[128:224].astype(BF16))
        gv_ref[:, sl] = dv[0:128] + mm(spread, dv[128:224].astype(BF16))
    row, col = iota2(PEERS * 8, 64)
    is_key = col < 32
    line = jnp.where(is_key, col, col - 32) + 16
    place = far_column(me, line) + jnp.where(is_key, 0, 2)
    first = mm(mat(row == place, 1.0), gf_ref[:, 0:HALF])
    second = mm(mat(row == place + 4, 1.0), gf_ref[:, HALF:WIDTH])
    slot_ref[:, 0:HALF] = (first + second).astype(BF16)
    slot_ref[:, HALF:] = jnp.zeros((PEERS * 8, 128), BF16)


def slope_kernel(s_ref, cross_ref, g5_ref, slot_in, five_ref, slot_out, tile_ref, sem):
    value = jnp.sum(jnp.sum(s_ref[...], axis=0), axis=1, keepdims=True)
    high, middle, low = three_parts(value)
    lane = lax.broadcasted_iota(jnp.int32, (HEADS, 128), 1)
    tile = jnp.where(
        lane == 0, high, jnp.where(lane == 1, middle, jnp.where(lane == 2, low, 0.0))
    )
    tile_ref[...] = jnp.concatenate([tile] * PEERS, axis=0).astype(BF16)
    put = pltpu.make_async_copy(tile_ref, slot_out.at[:, pl.ds(HALF, 128)], sem)
    put.start()
    five_ref[0:16, :] = g5_ref[...]
    five_ref[16:32, :] = cross_ref[32:48, :]
    put.wait()


def pair_kernel(g3_ref, cross_ref, five_ref, out_ref):
    at = ((lax.axis_index("seq") & 1) ^ 1) * 4
    out_ref[0:32, :] = g3_ref[...]
    out_ref[32:48, :] = cross_ref[16:32, :]
    row, col = iota2(16, 32)
    source = ((row >> 2) & 1) * 16 + (row >> 3) * 8 + at + (row & 3)
    out_ref[48:64, :] = mm(mat(col == source, 1.0), five_ref[...]).astype(BF16)


def final_kernel(
    gk_ref, gv_ref, pair_ref, cross_ref, five_ref, r_ref, ok_ref, ov_ref, os_ref
):
    me = lax.axis_index("seq")
    row, col = iota2(TOKENS, PEERS * 8)
    apart = (col >> 3) ^ me
    line = col & 7
    shift = jnp.where(apart >= 16, 7, 6)
    weight = jnp.where(apart >= 16, 2.0**-7, jnp.where(apart >= 8, 2.0**-6, 0.0))
    covers = lax.shift_right_logical(row, shift)
    row1, col1 = iota2(TOKENS, 64)
    row2, col2 = iota2(TOKENS, 48)
    row5, col5 = iota2(TOKENS, 32)
    for out_ref, own_ref, which in ((ok_ref, gk_ref, 0), (ov_ref, gv_ref, 1)):
        near = own_ref[...]
        three = jnp.where((row1 >> 3) + 16 * which == col1, 2.0**-3, 0.0)
        four = jnp.where((row1 >> 4) + 32 + 8 * which == col1, 2.0**-4, 0.0)
        held = (col1 >> 3) == 6 + which
        five = jnp.where(held & ((row1 >> 5) == (col1 & 3)), 2.0**-5, 0.0)
        near += mm((three + four + five).astype(BF16), pair_ref[...])
        near += mm(mat((row2 >> 4) + 8 * which == col2, 2.0**-4), cross_ref[...])
        held = ((col5 >> 3) & 1) == which
        mine = held & ((col5 & 7) == (me & 1) * 4 + (row5 >> 5))
        near += mm(mat(mine, 2.0**-5), five_ref[...])
        for half in range(2):
            sl = slice(HALF * half, HALF * half + HALF)
            far = mat(covers + 2 * which + 4 * half == line, weight)
            out_ref[:, sl] = (near[:, sl] + mm(far, r_ref[:, 0:HALF])).astype(BF16)
    slopes = r_ref[:, HALF:].astype(F32).reshape(PEERS, HEADS, 128)
    value = jnp.sum(jnp.sum(slopes, axis=0), axis=1, keepdims=True)
    srow, scol = iota2(HEADS, 128)
    line = jnp.sum(jnp.where(srow == scol, value, 0.0), axis=0, keepdims=True)
    os_ref[...] = line[:, 0:HEADS]


def call(kernel, outs, ins, places=None, out_places=None, scratch=(), cost=1 << 20, alias=None, vmem=12):
    places = places or [pltpu.VMEM] * len(ins)
    out_places = out_places or [pltpu.VMEM] * len(outs)
    return pl.pallas_call(
        kernel,
        out_shape=[jax.ShapeDtypeStruct(s, t) for s, t in outs],
        in_specs=[pl.BlockSpec(memory_space=place) for place in places],
        out_specs=[pl.BlockSpec(memory_space=place) for place in out_places],
        scratch_shapes=list(scratch),
        input_output_aliases=alias or {},
        compiler_params=pltpu.CompilerParams(vmem_limit_bytes=vmem * 1024 * 1024),
        cost_estimate=pl.CostEstimate(flops=0, bytes_accessed=cost, transcendentals=0),
    )(*ins)


def swap(block, apart):
    return lax.ppermute(block, "seq", [(i, i ^ apart) for i in range(PEERS)])


def exchange(slots):
    width = slots.shape[-1]
    back = lax.all_to_all(slots.reshape(PEERS, 8, width), "seq", 0, 0)
    return back.reshape(PEERS * 8, width)


def per_device(queries, keys_in, values_in, cotangent, level_slope):
    q, k, v, c = queries[0], keys_in[0], values_in[0], cotangent[0]
    wide = WIDTH
    block = pltpu.VMEM((TOKENS, wide), BF16)
    low, l3, l4, slots = call(
        pool_kernel,
        [((STEP + 16, wide), BF16), ((32, wide), BF16), ((16, wide), BF16), ((PEERS, 8, wide), BF16)],
        (k, v, level_slope),
        [pl.ANY] * 3,
        scratch=[block, block, pltpu.SMEM((HEADS,), F32), pltpu.SemaphoreType.DMA((3,))],
        vmem=58,
    )
    far = exchange(slots)
    near3 = swap(l3, 1)
    near4a = swap(l4, 2)
    near4b = swap(l4, 3)
    loc, near = call(
        local_kernel,
        [((STEPS + 16, wide), BF16), ((128, wide), F32)],
        (q, c, k, v, low),
        [pl.ANY] * 4 + [pltpu.VMEM],
        scratch=[pltpu.VMEM((LOCAL, wide), BF16), pltpu.SemaphoreType.DMA((4,))],
        cost=LONG,
    )
    groups = lax.axis_size("dp")
    work, slopes = call(
        score_kernel,
        [((DSCORES + KEYS, wide), BF16), ((groups, HEADS, 128), F32)],
        (loc, near, near3, near4a, near4b, far),
    )
    slopes = lax.all_to_all(slopes, "dp", 0, 0)
    g3, cross, g5, gf = call(
        far_grad_kernel,
        [((32, wide), BF16), ((48, wide), BF16), ((16, wide), BF16), ((64, wide), BF16)],
        (loc, work),
    )
    cross = swap(cross, 2)
    dq, gk, gv, slots = call(
        grad_kernel,
        [((TOKENS, wide), BF16), ((TOKENS, wide), F32), ((TOKENS, wide), F32),
         ((PEERS * 8, HALF + 128), BF16)],
        (loc, work, gf),
        cost=LONG,
    )
    five, slots = call(
        slope_kernel,
        [((32, wide), BF16), ((PEERS * 8, HALF + 128), BF16)],
        (slopes, cross, g5, slots),
        [pltpu.VMEM] * 3 + [pl.ANY],
        [pltpu.VMEM, pl.ANY],
        [pltpu.VMEM((PEERS * 8, 128), BF16), pltpu.SemaphoreType.DMA(())],
        alias={3: 1},
    )
    far = exchange(slots)
    five = swap(five, 4)
    (pair,) = call(pair_kernel, [((64, wide), BF16)], (g3, cross, five))
    pair = swap(pair, 1)
    dk, dv, ds = call(
        final_kernel,
        [((TOKENS, wide), BF16), ((TOKENS, wide), BF16), ((1, HEADS), F32)],
        (gk, gv, pair, cross, five, far),
    )
    return dq[None], dk[None], dv[None], ds.reshape(HEADS)


def solution(mesh):
    row = P("dp", "seq", None)
    return jax.shard_map(
        per_device,
        mesh=mesh,
        in_specs=(row, row, row, row, P()),
        out_specs=(row, row, row, P()),
        check_vma=False,
    )
```

```python
import math

import jax
import jax.numpy as jnp
from jax import lax
from jax.experimental import pallas as pl
from jax.experimental.pallas import tpu as pltpu
from jax.sharding import PartitionSpec as P

LOG_TWO = math.log(2.0)
HEADS = 8
HEAD_DIM = 128
WIDTH = HEADS * HEAD_DIM
TOKENS = 128
PEERS = 32
LEVELS = 8
KEYS = 144
FAR = 48
SCALE = 1.0 / math.sqrt(HEAD_DIM)
LONG = 1 << 28
F32 = jnp.float32
BF16 = jnp.bfloat16


def iota2(rows, cols):
    row = lax.broadcasted_iota(jnp.int32, (rows, cols), 0)
    col = lax.broadcasted_iota(jnp.int32, (rows, cols), 1)
    return row, col


def mat(mask, weight):
    return jnp.where(mask, weight, 0.0).astype(BF16)


def mm(left, right, dims=((1,), (0,))):
    return lax.dot_general(left, right, (dims, ((), ())), preferred_element_type=F32)


def pooling(rows, cols):
    row, col = iota2(rows, cols)
    return mat((col >> 1) == row, 0.5)


def three_parts(value):
    high = value.astype(BF16).astype(F32)
    rest = value - high
    middle = rest.astype(BF16).astype(F32)
    return high, middle, rest - middle


LOCAL = 224
REMOTE = 80
PROBS = 2 * REMOTE
DSCORES = PROBS + KEYS
HALF = WIDTH // 2
QUERY = LOCAL
COTANGENT = LOCAL + TOKENS
STEPS = LOCAL + 2 * TOKENS


def pool_kernel(k_hbm, v_hbm, l3_ref, l4_ref, slot_ref, k_ref, v_ref, sems):
    me = lax.axis_index("seq")
    fetch_k = pltpu.make_async_copy(k_hbm, k_ref, sems.at[0])
    fetch_v = pltpu.make_async_copy(v_hbm, v_ref, sems.at[1])
    fetch_k.start()
    fetch_v.start()
    half = pooling(64, 128)
    quarter = pooling(32, 64)
    l2 = []
    for fetch, held in ((fetch_k, k_ref), (fetch_v, v_ref)):
        fetch.wait()
        one = mm(half, held[...]).astype(BF16)
        l2.append(mm(quarter, one).astype(BF16))
    l3 = mm(quarter, jnp.concatenate(l2, axis=0)).astype(BF16)
    l3_ref[...] = l3
    l4 = mm(pooling(16, 32), l3).astype(BF16)
    l4_ref[...] = l4
    row, col = iota2(16, 16)
    l5 = mm(pooling(16, 16), l4).astype(BF16)
    m6 = mat((row < 8) & ((row & 3) < 2) & ((col >> 1) == ((row >> 2) * 2 + (row & 3))), 0.5)
    l6 = mm(m6, l5).astype(BF16)
    m7 = mat((row < 8) & ((row & 3) == 0) & ((col >> 1) == (row >> 1)), 0.5)
    l7 = mm(m7, l6).astype(BF16)
    b5, b6, b7 = l5[0:8], l6[0:8], l7[0:8]
    base7 = ((me >> 4) ^ 1) << 4
    base6 = ((me >> 3) ^ 1) << 3
    base5 = ((me >> 2) ^ 1) << 2
    base4 = (me >> 2) << 2
    for i in range(16):
        slot_ref[base7 + i] = b7
    for i in range(8):
        slot_ref[base6 + i] = b6
    for i in range(4):
        slot_ref[base5 + i] = b5
    for i in range(4):
        slot_ref[base4 + i] = jnp.zeros((8, WIDTH), BF16)


def far_column(me, line):
    at5 = ((((me >> 2) ^ 1) << 2) + (line >> 2)) * 8 + (line & 3)
    six = line - 16
    at6 = ((((me >> 3) ^ 1) << 3) + (six >> 1)) * 8 + (six & 1)
    at7 = ((((me >> 4) ^ 1) << 4) + (line - 32)) * 8
    return jnp.where(line < 16, at5, jnp.where(line < 32, at6, at7))


def local_kernel(q_hbm, c_hbm, k_hbm, v_hbm, slope_hbm, loc_ref, s_ref, v_ref, slope_ref, sems):
    moves = (
        (k_hbm, loc_ref.at[pl.ds(0, TOKENS)]),
        (q_hbm, loc_ref.at[pl.ds(QUERY, TOKENS)]),
        (v_hbm, v_ref.at[pl.ds(0, TOKENS)]),
        (c_hbm, loc_ref.at[pl.ds(COTANGENT, TOKENS)]),
        (slope_hbm, slope_ref),
    )
    fetches = [pltpu.make_async_copy(a, b, sems.at[i]) for i, (a, b) in enumerate(moves)]
    for fetch in fetches:
        fetch.start()
    part_at = lax.broadcasted_iota(jnp.int32, (16, HEAD_DIM), 0)
    fetches[4].wait()
    for h in range(HEADS):
        high, middle, low = three_parts(jnp.full((16, HEAD_DIM), LOG_TWO + slope_ref[h], F32))
        part = jnp.where(part_at == 1, middle, jnp.where(part_at == 2, low, 0.0))
        part = jnp.where(part_at == 0, high, part)
        loc_ref[STEPS : STEPS + 16, h * HEAD_DIM : (h + 1) * HEAD_DIM] = part.astype(BF16)
    lane = lax.broadcasted_iota(jnp.int32, (1, TOKENS), 1)
    quarter = lane >> 5
    lower = lane < 64


    def compact(full):
        def by_quarter(blocks):
            return jnp.where(
                quarter < 2,
                jnp.where(quarter == 0, blocks[0], blocks[1]),
                jnp.where(quarter == 2, blocks[2], blocks[3]),
            )

        zero = by_quarter([full[32 * g : 32 * g + 32] for g in range(4)])
        one = by_quarter([full[128 + 16 * (g ^ 1) : 144 + 16 * (g ^ 1)] for g in range(4)])
        two = jnp.where(lower, full[208:224], full[192:208])
        return zero, one, two

    step_all = jnp.sum(loc_ref[STEPS : STEPS + 16, :].astype(F32), axis=0, keepdims=True)
    half_mat, quarter_mat = pooling(64, 128), pooling(32, 64)
    for which, (held, at) in enumerate(((loc_ref, QUERY), (v_ref, COTANGENT))):
        fetches[2 * which].wait()
        one = mm(half_mat, held[0:TOKENS, :]).astype(BF16)
        held[TOKENS : TOKENS + 64, :] = one
        held[TOKENS + 64 : LOCAL, :] = mm(quarter_mat, one).astype(BF16)
        fetches[2 * which + 1].wait()
        for h in range(HEADS):
            sl = slice(h * HEAD_DIM, (h + 1) * HEAD_DIM)
            raw = mm(held[0:LOCAL, sl], loc_ref[at : at + TOKENS, sl], ((1,), (1,)))
            zero, one, two = compact(raw)
            if which == 0:
                step = step_all[:, sl]
                zero, one, two = zero * SCALE, one * SCALE + step, two * SCALE + 2 * step
            s_ref[64 * which : 64 * which + 64, sl] = jnp.concatenate([zero, one, two], axis=0)


def score_kernel(loc_ref, near_ref, r3_ref, r4a_ref, r4b_ref, r_ref, w_ref, s_ref):
    me = lax.axis_index("seq")
    row, col = iota2(FAR, PEERS * 8)
    place = far_column(me, row)
    far = r_ref[...]
    prow, pcol = iota2(16, 16)
    for which in range(2):
        at = REMOTE * which
        w_ref[at : at + 16, :] = r3_ref[16 * which : 16 * which + 16, :]
        first = mat((prow < 8) & (pcol == prow + 8 * which), 1.0)
        second = mat((prow >= 8) & (pcol == prow - 8 + 8 * which), 1.0)
        four = mm(first, r4a_ref[...]) + mm(second, r4b_ref[...])
        w_ref[at + 16 : at + 32, :] = four.astype(BF16)
        w_ref[at + 32 : at + 80, :] = mm(mat(col == place + 4 * which, 1.0), far).astype(BF16)
    step_all = jnp.sum(loc_ref[STEPS : STEPS + 16, :].astype(F32), axis=0, keepdims=True)
    total = [None] * HEADS
    for h in range(HEADS):
        sl = slice(h * HEAD_DIM, (h + 1) * HEAD_DIM)
        raw = mm(w_ref[0:REMOTE, sl], loc_ref[QUERY : QUERY + TOKENS, sl], ((1,), (1,)))
        step = step_all[:, sl]
        parts = [near_ref[0:64, sl]]
        parts += [raw[16 * i : 16 * i + 16] * SCALE + (i + 3) * step for i in range(5)]
        scores = jnp.concatenate(parts, axis=0)
        top = jnp.max(scores, axis=0, keepdims=True)
        expo = jnp.exp(scores - top)
        probs = expo * (1.0 / jnp.sum(expo, axis=0, keepdims=True))
        probs_b = probs.astype(BF16)
        raw = mm(w_ref[REMOTE : 2 * REMOTE, sl], loc_ref[COTANGENT : COTANGENT + TOKENS, sl], ((1,), (1,)))
        dprobs = jnp.concatenate([near_ref[64:128, sl], raw], axis=0)
        delta = jnp.sum(probs_b.astype(F32) * dprobs, axis=0, keepdims=True)
        dscores = probs * (dprobs - delta)
        w_ref[PROBS : PROBS + KEYS, sl] = probs_b
        w_ref[DSCORES : DSCORES + KEYS, sl] = dscores.astype(BF16)
        acc = None
        for level in range(1, LEVELS):
            at = 16 + 16 * level
            term = level * (dscores[at : at + 8] + dscores[at + 8 : at + 16])
            acc = term if acc is None else acc + term
        total[h] = jnp.sum(acc, axis=0, keepdims=True)
    tile = jnp.concatenate(total, axis=0)
    for i in range(s_ref.shape[0]):
        s_ref[i] = tile


def far_grad_kernel(loc_ref, w_ref, g3_ref, g4a_ref, g4b_ref, g5_ref, gf_ref):
    for h in range(HEADS):
        sl = slice(h * HEAD_DIM, (h + 1) * HEAD_DIM)
        q, c = loc_ref[QUERY : QUERY + TOKENS, sl], loc_ref[COTANGENT : COTANGENT + TOKENS, sl]
        dk = mm(w_ref[DSCORES + 64 : DSCORES + KEYS, sl], q) * SCALE
        dv = mm(w_ref[PROBS + 64 : PROBS + KEYS, sl], c)
        g3_ref[0:16, sl] = dk[0:16].astype(BF16)
        g3_ref[16:32, sl] = dv[0:16].astype(BF16)
        g4a_ref[:, sl] = jnp.concatenate([dk[16:24], dv[16:24]], axis=0).astype(BF16)
        g4b_ref[:, sl] = jnp.concatenate([dk[24:32], dv[24:32]], axis=0).astype(BF16)
        g5_ref[0:16, sl] = dk[32:48].astype(BF16)
        g5_ref[16:32, sl] = dv[32:48].astype(BF16)
        gf_ref[0:32, sl] = dk[48:80].astype(BF16)
        gf_ref[32:64, sl] = dv[48:80].astype(BF16)


def grad_kernel(loc_ref, w_ref, gf_ref, dq_ref, gk_ref, gv_ref, slot_ref):
    me = lax.axis_index("seq")
    lane = lax.broadcasted_iota(jnp.int32, (1, TOKENS), 1)
    quarter = lane >> 5
    lower = lane < 64

    srow, scol = iota2(TOKENS, 96)
    spread = jnp.where(
        (scol < 64) & (scol == (srow >> 1)),
        0.5,
        jnp.where((scol >= 64) & (scol - 64 == (srow >> 2)), 0.25, 0.0),
    ).astype(BF16)

    def expand(part):
        part = part.astype(F32)
        zero, one, two = part[0:32], part[32:48], part[48:64]
        rows = [jnp.where(quarter == g, zero, 0.0) for g in range(4)]
        rows += [jnp.where(quarter == (g ^ 1), one, 0.0) for g in range(4)]
        rows += [jnp.where(lower, 0.0, two), jnp.where(lower, two, 0.0)]
        return jnp.concatenate(rows, axis=0).astype(BF16)

    for h in range(HEADS):
        sl = slice(h * HEAD_DIM, (h + 1) * HEAD_DIM)
        q, c = loc_ref[QUERY : QUERY + TOKENS, sl], loc_ref[COTANGENT : COTANGENT + TOKENS, sl]
        d_near = expand(w_ref[DSCORES : DSCORES + 64, sl])
        p_near = expand(w_ref[PROBS : PROBS + 64, sl])
        d_far = w_ref[DSCORES + 64 : DSCORES + KEYS, sl]
        dq = mm(d_near, loc_ref[0:LOCAL, sl], ((0,), (0,))) + mm(d_far, w_ref[0:REMOTE, sl], ((0,), (0,)))
        dq_ref[:, sl] = (dq * SCALE).astype(BF16)
        dk = mm(d_near, q) * SCALE
        dv = mm(p_near, c)
        gk_ref[:, sl] = dk[0:128] + mm(spread, dk[128:224].astype(BF16))
        gv_ref[:, sl] = dv[0:128] + mm(spread, dv[128:224].astype(BF16))
    row, col = iota2(PEERS * 8, 64)
    is_key = col < 32
    line = jnp.where(is_key, col, col - 32) + 16
    place = far_column(me, line) + jnp.where(is_key, 0, 2)
    first = mm(mat(row == place, 1.0), gf_ref[:, 0:HALF])
    second = mm(mat(row == place + 4, 1.0), gf_ref[:, HALF:WIDTH])
    slot_ref[:, 0:HALF] = (first + second).astype(BF16)
    slot_ref[:, HALF:] = jnp.zeros((PEERS * 8, 128), BF16)


def slope_kernel(
    s_ref, r5_ref, g3_ref, g4a_ref, g4b_ref, slot_in, pair_ref, a_ref, b_ref, slot_out, tile_ref, sem
):
    me = lax.axis_index("seq")
    value = jnp.sum(jnp.sum(s_ref[...], axis=0), axis=1, keepdims=True)
    high, middle, low = three_parts(value)
    lane = lax.broadcasted_iota(jnp.int32, (HEADS, 128), 1)
    tile = jnp.where(
        lane == 0, high, jnp.where(lane == 1, middle, jnp.where(lane == 2, low, 0.0))
    )
    tile_ref[...] = jnp.concatenate([tile] * PEERS, axis=0).astype(BF16)
    put = pltpu.make_async_copy(tile_ref, slot_out.at[:, pl.ds(HALF, 128)], sem)
    put.start()
    row, col = iota2(16, 32)
    for apart, own_ref, out_ref in ((1, g3_ref, pair_ref), (2, g4a_ref, a_ref), (3, g4b_ref, b_ref)):
        size = own_ref.shape[0]
        out_ref[0:size, :] = own_ref[...]
        at = ((me & 3) ^ apart) * 4
        pick = ((row < 4) & (col == at + row)) | ((row >= 4) & (row < 8) & (col == at + row + 12))
        out_ref[size : size + 16, :] = mm(mat(pick, 1.0), r5_ref[...]).astype(BF16)
    put.wait()


def final_kernel(
    gk_ref, gv_ref, pair_ref, a_ref, b_ref, r5_ref, r_ref, ok_ref, ov_ref, os_ref
):
    me = lax.axis_index("seq")
    row, col = iota2(TOKENS, PEERS * 8)
    apart = (col >> 3) ^ me
    line = col & 7
    shift = jnp.where(apart >= 16, 7, 6)
    weight = jnp.where(apart >= 16, 2.0**-7, jnp.where(apart >= 8, 2.0**-6, 0.0))
    covers = lax.shift_right_logical(row, shift)
    row3, col3 = iota2(TOKENS, 48)
    row4, col4 = iota2(TOKENS, 32)
    for out_ref, own_ref, which in ((ok_ref, gk_ref, 0), (ov_ref, gv_ref, 1)):
        near = own_ref[...]
        three = jnp.where((row3 >> 3) + 16 * which == col3, 2.0**-3, 0.0)
        five = jnp.where((row3 >> 5) + 32 + 4 * which == col3, 2.0**-5, 0.0)
        near += mm((three + five).astype(BF16), pair_ref[...])
        four = jnp.where((row4 >> 4) + 8 * which == col4, 2.0**-4, 0.0)
        five = jnp.where((row4 >> 5) + 16 + 4 * which == col4, 2.0**-5, 0.0)
        both = (four + five).astype(BF16)
        near += mm(both, a_ref[...]) + mm(both, b_ref[...])
        mine = mat((row4 >> 5) + 4 * (me & 3) + 16 * which == col4, 2.0**-5)
        near += mm(mine, r5_ref[...])
        for half in range(2):
            sl = slice(HALF * half, HALF * half + HALF)
            far = mat(covers + 2 * which + 4 * half == line, weight)
            out_ref[:, sl] = (near[:, sl] + mm(far, r_ref[:, 0:HALF])).astype(BF16)
    slopes = r_ref[:, HALF:].astype(F32).reshape(PEERS, HEADS, 128)
    value = jnp.sum(jnp.sum(slopes, axis=0), axis=1, keepdims=True)
    srow, scol = iota2(HEADS, 128)
    line = jnp.sum(jnp.where(srow == scol, value, 0.0), axis=0, keepdims=True)
    os_ref[...] = line[:, 0:HEADS]


def call(kernel, outs, ins, places=None, out_places=None, scratch=(), cost=1 << 20, alias=None, vmem=12):
    places = places or [pltpu.VMEM] * len(ins)
    out_places = out_places or [pltpu.VMEM] * len(outs)
    return pl.pallas_call(
        kernel,
        out_shape=[jax.ShapeDtypeStruct(s, t) for s, t in outs],
        in_specs=[pl.BlockSpec(memory_space=place) for place in places],
        out_specs=[pl.BlockSpec(memory_space=place) for place in out_places],
        scratch_shapes=list(scratch),
        input_output_aliases=alias or {},
        compiler_params=pltpu.CompilerParams(vmem_limit_bytes=vmem * 1024 * 1024),
        cost_estimate=pl.CostEstimate(flops=0, bytes_accessed=cost, transcendentals=0),
    )(*ins)


def swap(block, apart):
    return lax.ppermute(block, "seq", [(i, i ^ apart) for i in range(PEERS)])


def exchange(slots):
    width = slots.shape[-1]
    back = lax.all_to_all(slots.reshape(PEERS, 8, width), "seq", 0, 0)
    return back.reshape(PEERS * 8, width)


def per_device(queries, keys_in, values_in, cotangent, level_slope):
    q, k, v, c = queries[0], keys_in[0], values_in[0], cotangent[0]
    wide = WIDTH
    block = pltpu.VMEM((TOKENS, wide), BF16)
    l3, l4, slots = call(
        pool_kernel,
        [((32, wide), BF16), ((16, wide), BF16), ((PEERS, 8, wide), BF16)],
        (k, v),
        [pl.ANY] * 2,
        scratch=[block, block, pltpu.SemaphoreType.DMA((2,))],
        vmem=58,
    )
    far = exchange(slots)
    near3 = swap(l3, 1)
    near4a = swap(l4, 2)
    near4b = swap(l4, 3)
    loc, near = call(
        local_kernel,
        [((STEPS + 16, wide), BF16), ((128, wide), F32)],
        (q, c, k, v, level_slope),
        [pl.ANY] * 5,
        scratch=[pltpu.VMEM((LOCAL, wide), BF16), pltpu.SMEM((HEADS,), F32),
                 pltpu.SemaphoreType.DMA((5,))],
        cost=LONG,
    )
    groups = lax.axis_size("dp")
    work, slopes = call(
        score_kernel,
        [((DSCORES + KEYS, wide), BF16), ((groups, HEADS, 128), F32)],
        (loc, near, near3, near4a, near4b, far),
    )
    slopes = lax.all_to_all(slopes, "dp", 0, 0)
    g3, g4a, g4b, g5, gf = call(
        far_grad_kernel,
        [((32, wide), BF16), ((16, wide), BF16), ((16, wide), BF16), ((32, wide), BF16), ((64, wide), BF16)],
        (loc, work),
    )
    near5 = swap(g5, 4)
    dq, gk, gv, slots = call(
        grad_kernel,
        [((TOKENS, wide), BF16), ((TOKENS, wide), F32), ((TOKENS, wide), F32),
         ((PEERS * 8, HALF + 128), BF16)],
        (loc, work, gf),
        cost=LONG,
    )
    pair, four_a, four_b, slots = call(
        slope_kernel,
        [((48, wide), BF16), ((32, wide), BF16), ((32, wide), BF16), ((PEERS * 8, HALF + 128), BF16)],
        (slopes, near5, g3, g4a, g4b, slots),
        [pltpu.VMEM] * 5 + [pl.ANY],
        [pltpu.VMEM] * 3 + [pl.ANY],
        [pltpu.VMEM((PEERS * 8, 128), BF16), pltpu.SemaphoreType.DMA(())],
        alias={5: 3},
    )
    far = exchange(slots)
    pair = swap(pair, 1)
    four_a = swap(four_a, 2)
    four_b = swap(four_b, 3)
    dk, dv, ds = call(
        final_kernel,
        [((TOKENS, wide), BF16), ((TOKENS, wide), BF16), ((1, HEADS), F32)],
        (gk, gv, pair, four_a, four_b, near5, far),
    )
    return dq[None], dk[None], dv[None], ds.reshape(HEADS)


def solution(mesh):
    row = P("dp", "seq", None)
    return jax.shard_map(
        per_device,
        mesh=mesh,
        in_specs=(row, row, row, row, P()),
        out_specs=(row, row, row, P()),
        check_vma=False,
    )
```

```python
import math

import jax
import jax.numpy as jnp
from jax import lax
from jax.experimental import pallas as pl
from jax.experimental.pallas import tpu as pltpu
from jax.sharding import PartitionSpec as P

LOG_TWO = math.log(2.0)
HEADS = 8
HEAD_DIM = 128
WIDTH = HEADS * HEAD_DIM
TOKENS = 128
PEERS = 32
LEVELS = 8
KEYS = 144
FAR = 48
SCALE = 1.0 / math.sqrt(HEAD_DIM)
LONG = 1 << 28
F32 = jnp.float32
BF16 = jnp.bfloat16


def iota2(rows, cols):
    row = lax.broadcasted_iota(jnp.int32, (rows, cols), 0)
    col = lax.broadcasted_iota(jnp.int32, (rows, cols), 1)
    return row, col


def mat(mask, weight):
    return jnp.where(mask, weight, 0.0).astype(BF16)


def mm(left, right, dims=((1,), (0,))):
    return lax.dot_general(left, right, (dims, ((), ())), preferred_element_type=F32)


def pooling(rows, cols):
    row, col = iota2(rows, cols)
    return mat((col >> 1) == row, 0.5)


def three_parts(value):
    high = value.astype(BF16).astype(F32)
    rest = value - high
    middle = rest.astype(BF16).astype(F32)
    return high, middle, rest - middle


LOCAL = 224
REMOTE = 80
PROBS = 2 * REMOTE
DSCORES = PROBS + KEYS
HALF = WIDTH // 2
QUERY = LOCAL
COTANGENT = LOCAL + TOKENS
STEPS = LOCAL + 2 * TOKENS


def pool_kernel(k_hbm, v_hbm, l3_ref, l4_ref, slot_hbm, k_ref, v_ref, slot_ref, sems):
    me = lax.axis_index("seq")
    fetches = []
    for source, held in ((k_hbm, k_ref), (v_hbm, v_ref)):
        for rows in (pl.ds(0, 64), pl.ds(64, 64)):
            sem = sems.at[len(fetches)]
            fetches.append(pltpu.make_async_copy(source.at[rows], held.at[rows], sem))
            fetches[-1].start()
    half = pooling(64, 128)
    quarter = pooling(32, 64)
    l2 = []
    for i, held in enumerate((k_ref, v_ref)):
        fetches[2 * i].wait()
        fetches[2 * i + 1].wait()
        one = mm(half, held[...]).astype(BF16)
        l2.append(mm(quarter, one).astype(BF16))
    l3 = mm(quarter, jnp.concatenate(l2, axis=0)).astype(BF16)
    l3_ref[...] = l3
    l4 = mm(pooling(16, 32), l3).astype(BF16)
    l4_ref[...] = l4
    row, col = iota2(16, 16)
    puts = []

    def put(at):
        rows = pl.ds(at, 8)
        puts.append(pltpu.make_async_copy(slot_ref.at[rows], slot_hbm.at[rows], sems.at[4 + len(puts)]))
        puts[-1].start()

    base7 = ((me >> 4) ^ 1) << 4
    base6 = ((me >> 3) ^ 1) << 3
    base5 = ((me >> 2) ^ 1) << 2
    base4 = (me >> 2) << 2
    l5 = mm(pooling(16, 16), l4).astype(BF16)
    for i in range(4):
        slot_ref[base5 + i] = l5[0:8]
        slot_ref[base4 + i] = jnp.zeros((8, WIDTH), BF16)
    put((me >> 3) << 3)
    m6 = mat((row < 8) & ((row & 3) < 2) & ((col >> 1) == ((row >> 2) * 2 + (row & 3))), 0.5)
    l6 = mm(m6, l5).astype(BF16)
    for i in range(8):
        slot_ref[base6 + i] = l6[0:8]
    put(base6)
    m7 = mat((row < 8) & ((row & 3) == 0) & ((col >> 1) == (row >> 1)), 0.5)
    l7 = mm(m7, l6).astype(BF16)
    for i in range(8):
        slot_ref[base7 + i] = l7[0:8]
    put(base7)
    for i in range(8, 16):
        slot_ref[base7 + i] = l7[0:8]
    put(base7 + 8)
    for copy in puts:
        copy.wait()


def far_column(me, line):
    at5 = ((((me >> 2) ^ 1) << 2) + (line >> 2)) * 8 + (line & 3)
    six = line - 16
    at6 = ((((me >> 3) ^ 1) << 3) + (six >> 1)) * 8 + (six & 1)
    at7 = ((((me >> 4) ^ 1) << 4) + (line - 32)) * 8
    return jnp.where(line < 16, at5, jnp.where(line < 32, at6, at7))


def local_kernel(q_hbm, c_hbm, k_hbm, v_hbm, slope_hbm, loc_ref, s_ref, v_ref, slope_ref, sems):
    moves = (
        (k_hbm, loc_ref.at[pl.ds(0, TOKENS)]),
        (q_hbm, loc_ref.at[pl.ds(QUERY, TOKENS)]),
        (v_hbm, v_ref.at[pl.ds(0, TOKENS)]),
        (c_hbm, loc_ref.at[pl.ds(COTANGENT, TOKENS)]),
        (slope_hbm, slope_ref),
    )
    fetches = [pltpu.make_async_copy(a, b, sems.at[i]) for i, (a, b) in enumerate(moves)]
    for fetch in fetches:
        fetch.start()
    part_at = lax.broadcasted_iota(jnp.int32, (16, HEAD_DIM), 0)
    fetches[4].wait()
    for h in range(HEADS):
        high, middle, low = three_parts(jnp.full((16, HEAD_DIM), LOG_TWO + slope_ref[h], F32))
        part = jnp.where(part_at == 1, middle, jnp.where(part_at == 2, low, 0.0))
        part = jnp.where(part_at == 0, high, part)
        loc_ref[STEPS : STEPS + 16, h * HEAD_DIM : (h + 1) * HEAD_DIM] = part.astype(BF16)
    lane = lax.broadcasted_iota(jnp.int32, (1, TOKENS), 1)
    quarter = lane >> 5
    lower = lane < 64


    def compact(full):
        def by_quarter(blocks):
            return jnp.where(
                quarter < 2,
                jnp.where(quarter == 0, blocks[0], blocks[1]),
                jnp.where(quarter == 2, blocks[2], blocks[3]),
            )

        zero = by_quarter([full[32 * g : 32 * g + 32] for g in range(4)])
        one = by_quarter([full[128 + 16 * (g ^ 1) : 144 + 16 * (g ^ 1)] for g in range(4)])
        two = jnp.where(lower, full[208:224], full[192:208])
        return zero, one, two

    step_all = jnp.sum(loc_ref[STEPS : STEPS + 16, :].astype(F32), axis=0, keepdims=True)
    half_mat, quarter_mat = pooling(64, 128), pooling(32, 64)
    for which, (held, at) in enumerate(((loc_ref, QUERY), (v_ref, COTANGENT))):
        fetches[2 * which].wait()
        one = mm(half_mat, held[0:TOKENS, :]).astype(BF16)
        held[TOKENS : TOKENS + 64, :] = one
        held[TOKENS + 64 : LOCAL, :] = mm(quarter_mat, one).astype(BF16)
        fetches[2 * which + 1].wait()
        for h in range(HEADS):
            sl = slice(h * HEAD_DIM, (h + 1) * HEAD_DIM)
            raw = mm(held[0:LOCAL, sl], loc_ref[at : at + TOKENS, sl], ((1,), (1,)))
            zero, one, two = compact(raw)
            if which == 0:
                step = step_all[:, sl]
                zero, one, two = zero * SCALE, one * SCALE + step, two * SCALE + 2 * step
            s_ref[64 * which : 64 * which + 64, sl] = jnp.concatenate([zero, one, two], axis=0)


def score_kernel(loc_ref, near_ref, r3_ref, r4a_ref, r4b_ref, r_ref, w_ref, s_ref):
    me = lax.axis_index("seq")
    row, col = iota2(FAR, PEERS * 8)
    place = far_column(me, row)
    far = r_ref[...]
    prow, pcol = iota2(16, 16)
    for which in range(2):
        at = REMOTE * which
        w_ref[at : at + 16, :] = r3_ref[16 * which : 16 * which + 16, :]
        first = mat((prow < 8) & (pcol == prow + 8 * which), 1.0)
        second = mat((prow >= 8) & (pcol == prow - 8 + 8 * which), 1.0)
        four = mm(first, r4a_ref[...]) + mm(second, r4b_ref[...])
        w_ref[at + 16 : at + 32, :] = four.astype(BF16)
        w_ref[at + 32 : at + 80, :] = mm(mat(col == place + 4 * which, 1.0), far).astype(BF16)
    step_all = jnp.sum(loc_ref[STEPS : STEPS + 16, :].astype(F32), axis=0, keepdims=True)
    total = [None] * HEADS
    for h in range(HEADS):
        sl = slice(h * HEAD_DIM, (h + 1) * HEAD_DIM)
        raw = mm(w_ref[0:REMOTE, sl], loc_ref[QUERY : QUERY + TOKENS, sl], ((1,), (1,)))
        step = step_all[:, sl]
        parts = [near_ref[0:64, sl]]
        parts += [raw[16 * i : 16 * i + 16] * SCALE + (i + 3) * step for i in range(5)]
        scores = jnp.concatenate(parts, axis=0)
        top = jnp.max(scores, axis=0, keepdims=True)
        expo = jnp.exp(scores - top)
        probs = expo * (1.0 / jnp.sum(expo, axis=0, keepdims=True))
        probs_b = probs.astype(BF16)
        raw = mm(w_ref[REMOTE : 2 * REMOTE, sl], loc_ref[COTANGENT : COTANGENT + TOKENS, sl], ((1,), (1,)))
        dprobs = jnp.concatenate([near_ref[64:128, sl], raw], axis=0)
        delta = jnp.sum(probs_b.astype(F32) * dprobs, axis=0, keepdims=True)
        dscores = probs * (dprobs - delta)
        w_ref[PROBS : PROBS + KEYS, sl] = probs_b
        w_ref[DSCORES : DSCORES + KEYS, sl] = dscores.astype(BF16)
        acc = None
        for level in range(1, LEVELS):
            at = 16 + 16 * level
            term = level * (dscores[at : at + 8] + dscores[at + 8 : at + 16])
            acc = term if acc is None else acc + term
        total[h] = jnp.sum(acc, axis=0, keepdims=True)
    tile = jnp.concatenate(total, axis=0)
    for i in range(s_ref.shape[0]):
        s_ref[i] = tile


def far_grad_kernel(loc_ref, w_ref, g3_ref, g4a_ref, g4b_ref, g5_ref, gf_ref):
    for h in range(HEADS):
        sl = slice(h * HEAD_DIM, (h + 1) * HEAD_DIM)
        q, c = loc_ref[QUERY : QUERY + TOKENS, sl], loc_ref[COTANGENT : COTANGENT + TOKENS, sl]
        dk = mm(w_ref[DSCORES + 64 : DSCORES + KEYS, sl], q) * SCALE
        dv = mm(w_ref[PROBS + 64 : PROBS + KEYS, sl], c)
        g3_ref[0:16, sl] = dk[0:16].astype(BF16)
        g3_ref[16:32, sl] = dv[0:16].astype(BF16)
        g4a_ref[:, sl] = jnp.concatenate([dk[16:24], dv[16:24]], axis=0).astype(BF16)
        g4b_ref[:, sl] = jnp.concatenate([dk[24:32], dv[24:32]], axis=0).astype(BF16)
        g5_ref[0:16, sl] = dk[32:48].astype(BF16)
        g5_ref[16:32, sl] = dv[32:48].astype(BF16)
        gf_ref[0:32, sl] = dk[48:80].astype(BF16)
        gf_ref[32:64, sl] = dv[48:80].astype(BF16)


def grad_kernel(loc_ref, w_ref, gf_ref, dq_ref, gk_ref, gv_ref, slot_ref):
    me = lax.axis_index("seq")
    lane = lax.broadcasted_iota(jnp.int32, (1, TOKENS), 1)
    quarter = lane >> 5
    lower = lane < 64

    srow, scol = iota2(TOKENS, 96)
    spread = jnp.where(
        (scol < 64) & (scol == (srow >> 1)),
        0.5,
        jnp.where((scol >= 64) & (scol - 64 == (srow >> 2)), 0.25, 0.0),
    ).astype(BF16)

    def expand(part):
        part = part.astype(F32)
        zero, one, two = part[0:32], part[32:48], part[48:64]
        rows = [jnp.where(quarter == g, zero, 0.0) for g in range(4)]
        rows += [jnp.where(quarter == (g ^ 1), one, 0.0) for g in range(4)]
        rows += [jnp.where(lower, 0.0, two), jnp.where(lower, two, 0.0)]
        return jnp.concatenate(rows, axis=0).astype(BF16)

    for h in range(HEADS):
        sl = slice(h * HEAD_DIM, (h + 1) * HEAD_DIM)
        q, c = loc_ref[QUERY : QUERY + TOKENS, sl], loc_ref[COTANGENT : COTANGENT + TOKENS, sl]
        d_near = expand(w_ref[DSCORES : DSCORES + 64, sl])
        p_near = expand(w_ref[PROBS : PROBS + 64, sl])
        d_far = w_ref[DSCORES + 64 : DSCORES + KEYS, sl]
        dq = mm(d_near, loc_ref[0:LOCAL, sl], ((0,), (0,))) + mm(d_far, w_ref[0:REMOTE, sl], ((0,), (0,)))
        dq_ref[:, sl] = (dq * SCALE).astype(BF16)
        dk = mm(d_near, q) * SCALE
        dv = mm(p_near, c)
        gk_ref[:, sl] = dk[0:128] + mm(spread, dk[128:224].astype(BF16))
        gv_ref[:, sl] = dv[0:128] + mm(spread, dv[128:224].astype(BF16))
    row, col = iota2(PEERS * 8, 64)
    is_key = col < 32
    line = jnp.where(is_key, col, col - 32) + 16
    place = far_column(me, line) + jnp.where(is_key, 0, 2)
    first = mm(mat(row == place, 1.0), gf_ref[:, 0:HALF])
    second = mm(mat(row == place + 4, 1.0), gf_ref[:, HALF:WIDTH])
    slot_ref[:, 0:HALF] = (first + second).astype(BF16)
    slot_ref[:, HALF:] = jnp.zeros((PEERS * 8, 128), BF16)


def slope_kernel(
    s_ref, r5_ref, g3_ref, g4a_ref, g4b_ref, slot_in, pair_ref, a_ref, b_ref, slot_out, tile_ref, sem
):
    me = lax.axis_index("seq")
    value = jnp.sum(jnp.sum(s_ref[...], axis=0), axis=1, keepdims=True)
    high, middle, low = three_parts(value)
    lane = lax.broadcasted_iota(jnp.int32, (HEADS, 128), 1)
    tile = jnp.where(
        lane == 0, high, jnp.where(lane == 1, middle, jnp.where(lane == 2, low, 0.0))
    )
    tile_ref[...] = jnp.concatenate([tile] * PEERS, axis=0).astype(BF16)
    put = pltpu.make_async_copy(tile_ref, slot_out.at[:, pl.ds(HALF, 128)], sem)
    put.start()
    row, col = iota2(16, 32)
    for apart, own_ref, out_ref in ((1, g3_ref, pair_ref), (2, g4a_ref, a_ref), (3, g4b_ref, b_ref)):
        size = own_ref.shape[0]
        out_ref[0:size, :] = own_ref[...]
        at = ((me & 3) ^ apart) * 4
        pick = ((row < 4) & (col == at + row)) | ((row >= 4) & (row < 8) & (col == at + row + 12))
        out_ref[size : size + 16, :] = mm(mat(pick, 1.0), r5_ref[...]).astype(BF16)
    put.wait()


def final_kernel(
    gk_ref, gv_ref, pair_ref, a_ref, b_ref, r5_ref, r_ref, ok_hbm, ov_hbm, os_ref, ok_ref, ov_ref, sems
):
    me = lax.axis_index("seq")
    row, col = iota2(TOKENS, PEERS * 8)
    apart = (col >> 3) ^ me
    line = col & 7
    shift = jnp.where(apart >= 16, 7, 6)
    weight = jnp.where(apart >= 16, 2.0**-7, jnp.where(apart >= 8, 2.0**-6, 0.0))
    covers = lax.shift_right_logical(row, shift)
    row3, col3 = iota2(TOKENS, 48)
    row4, col4 = iota2(TOKENS, 32)
    puts = []
    for out_hbm, out_ref, own_ref, which in ((ok_hbm, ok_ref, gk_ref, 0), (ov_hbm, ov_ref, gv_ref, 1)):
        near = own_ref[...]
        three = jnp.where((row3 >> 3) + 16 * which == col3, 2.0**-3, 0.0)
        five = jnp.where((row3 >> 5) + 32 + 4 * which == col3, 2.0**-5, 0.0)
        near += mm((three + five).astype(BF16), pair_ref[...])
        four = jnp.where((row4 >> 4) + 8 * which == col4, 2.0**-4, 0.0)
        five = jnp.where((row4 >> 5) + 16 + 4 * which == col4, 2.0**-5, 0.0)
        both = (four + five).astype(BF16)
        near += mm(both, a_ref[...]) + mm(both, b_ref[...])
        mine = mat((row4 >> 5) + 4 * (me & 3) + 16 * which == col4, 2.0**-5)
        near += mm(mine, r5_ref[...])
        for half in range(2):
            sl = slice(HALF * half, HALF * half + HALF)
            far = mat(covers + 2 * which + 4 * half == line, weight)
            out_ref[:, sl] = (near[:, sl] + mm(far, r_ref[:, 0:HALF])).astype(BF16)
        for rows in (pl.ds(0, 64), pl.ds(64, 64)):
            sem = sems.at[len(puts)]
            puts.append(pltpu.make_async_copy(out_ref.at[rows], out_hbm.at[rows], sem))
            puts[-1].start()
    slopes = r_ref[:, HALF:].astype(F32).reshape(PEERS, HEADS, 128)
    value = jnp.sum(jnp.sum(slopes, axis=0), axis=1, keepdims=True)
    srow, scol = iota2(HEADS, 128)
    line = jnp.sum(jnp.where(srow == scol, value, 0.0), axis=0, keepdims=True)
    os_ref[...] = line[:, 0:HEADS]
    for copy in puts:
        copy.wait()


def call(kernel, outs, ins, places=None, out_places=None, scratch=(), cost=1 << 20, alias=None, vmem=12):
    places = places or [pltpu.VMEM] * len(ins)
    out_places = out_places or [pltpu.VMEM] * len(outs)
    return pl.pallas_call(
        kernel,
        out_shape=[jax.ShapeDtypeStruct(s, t) for s, t in outs],
        in_specs=[pl.BlockSpec(memory_space=place) for place in places],
        out_specs=[pl.BlockSpec(memory_space=place) for place in out_places],
        scratch_shapes=list(scratch),
        input_output_aliases=alias or {},
        compiler_params=pltpu.CompilerParams(vmem_limit_bytes=vmem * 1024 * 1024),
        cost_estimate=pl.CostEstimate(flops=0, bytes_accessed=cost, transcendentals=0),
    )(*ins)


def swap(block, apart):
    return lax.ppermute(block, "seq", [(i, i ^ apart) for i in range(PEERS)])


def exchange(slots):
    width = slots.shape[-1]
    back = lax.all_to_all(slots.reshape(PEERS, 8, width), "seq", 0, 0)
    return back.reshape(PEERS * 8, width)


def per_device(queries, keys_in, values_in, cotangent, level_slope):
    q, k, v, c = queries[0], keys_in[0], values_in[0], cotangent[0]
    wide = WIDTH
    block = pltpu.VMEM((TOKENS, wide), BF16)
    l3, l4, slots = call(
        pool_kernel,
        [((32, wide), BF16), ((16, wide), BF16), ((PEERS, 8, wide), BF16)],
        (k, v),
        [pl.ANY] * 2,
        [pltpu.VMEM, pltpu.VMEM, pl.ANY],
        [block, block, pltpu.VMEM((PEERS, 8, wide), BF16), pltpu.SemaphoreType.DMA((8,))],
        vmem=58,
    )
    far = exchange(slots)
    near3 = swap(l3, 1)
    near4a = swap(l4, 2)
    near4b = swap(l4, 3)
    loc, near = call(
        local_kernel,
        [((STEPS + 16, wide), BF16), ((128, wide), F32)],
        (q, c, k, v, level_slope),
        [pl.ANY] * 5,
        scratch=[pltpu.VMEM((LOCAL, wide), BF16), pltpu.SMEM((HEADS,), F32),
                 pltpu.SemaphoreType.DMA((5,))],
        cost=LONG,
    )
    groups = lax.axis_size("dp")
    work, slopes = call(
        score_kernel,
        [((DSCORES + KEYS, wide), BF16), ((groups, HEADS, 128), F32)],
        (loc, near, near3, near4a, near4b, far),
    )
    slopes = lax.all_to_all(slopes, "dp", 0, 0)
    g3, g4a, g4b, g5, gf = call(
        far_grad_kernel,
        [((32, wide), BF16), ((16, wide), BF16), ((16, wide), BF16), ((32, wide), BF16), ((64, wide), BF16)],
        (loc, work),
    )
    near5 = swap(g5, 4)
    dq, gk, gv, slots = call(
        grad_kernel,
        [((TOKENS, wide), BF16), ((TOKENS, wide), F32), ((TOKENS, wide), F32),
         ((PEERS * 8, HALF + 128), BF16)],
        (loc, work, gf),
        cost=LONG,
    )
    pair, four_a, four_b, slots = call(
        slope_kernel,
        [((48, wide), BF16), ((32, wide), BF16), ((32, wide), BF16), ((PEERS * 8, HALF + 128), BF16)],
        (slopes, near5, g3, g4a, g4b, slots),
        [pltpu.VMEM] * 5 + [pl.ANY],
        [pltpu.VMEM] * 3 + [pl.ANY],
        [pltpu.VMEM((PEERS * 8, 128), BF16), pltpu.SemaphoreType.DMA(())],
        alias={5: 3},
    )
    far = exchange(slots)
    pair = swap(pair, 1)
    four_a = swap(four_a, 2)
    four_b = swap(four_b, 3)
    dk, dv, ds = call(
        final_kernel,
        [((TOKENS, wide), BF16), ((TOKENS, wide), BF16), ((1, HEADS), F32)],
        (gk, gv, pair, four_a, four_b, near5, far),
        out_places=[pl.ANY, pl.ANY, pltpu.VMEM],
        scratch=[block, block, pltpu.SemaphoreType.DMA((4,))],
    )
    return dq[None], dk[None], dv[None], ds.reshape(HEADS)


def solution(mesh):
    row = P("dp", "seq", None)
    return jax.shard_map(
        per_device,
        mesh=mesh,
        in_specs=(row, row, row, row, P()),
        out_specs=(row, row, row, P()),
        check_vma=False,
    )
```

```python
import math

import jax
import jax.numpy as jnp
from jax import lax
from jax.experimental import pallas as pl
from jax.experimental.pallas import tpu as pltpu
from jax.sharding import PartitionSpec as P

LOG_TWO = math.log(2.0)
HEADS = 8
HEAD_DIM = 128
WIDTH = HEADS * HEAD_DIM
TOKENS = 128
PEERS = 32
LEVELS = 8
KEYS = 144
FAR = 48
SCALE = 1.0 / math.sqrt(HEAD_DIM)
LONG = 1 << 28
F32 = jnp.float32
BF16 = jnp.bfloat16


def iota2(rows, cols):
    row = lax.broadcasted_iota(jnp.int32, (rows, cols), 0)
    col = lax.broadcasted_iota(jnp.int32, (rows, cols), 1)
    return row, col


def mat(mask, weight):
    return jnp.where(mask, weight, 0.0).astype(BF16)


def mm(left, right, dims=((1,), (0,))):
    return lax.dot_general(left, right, (dims, ((), ())), preferred_element_type=F32)


def pooling(rows, cols):
    row, col = iota2(rows, cols)
    return mat((col >> 1) == row, 0.5)


def three_parts(value):
    high = value.astype(BF16).astype(F32)
    rest = value - high
    middle = rest.astype(BF16).astype(F32)
    return high, middle, rest - middle


LOCAL = 224
COARSE = 96
STEP = 2 * COARSE
REMOTE = 80
PROBS = 2 * REMOTE
DSCORES = PROBS + KEYS
HALF = WIDTH // 2
QUERY = LOCAL
COTANGENT = LOCAL + TOKENS
STEPS = LOCAL + 2 * TOKENS


def pool_kernel(
    k_hbm, v_hbm, slope_hbm, low_ref, l3_ref, l4_ref, slot_ref, k_ref, v_ref, slope_ref, sems
):
    me = lax.axis_index("seq")
    fetch_k = pltpu.make_async_copy(k_hbm, k_ref, sems.at[0])
    fetch_v = pltpu.make_async_copy(v_hbm, v_ref, sems.at[1])
    fetch_slope = pltpu.make_async_copy(slope_hbm, slope_ref, sems.at[2])
    fetch_k.start()
    fetch_v.start()
    fetch_slope.start()
    half = pooling(64, 128)
    quarter = pooling(32, 64)
    fetch_slope.wait()
    line = lax.broadcasted_iota(jnp.int32, (16, HEAD_DIM), 0)
    for h in range(HEADS):
        high, middle, low = three_parts(jnp.full((16, HEAD_DIM), LOG_TWO + slope_ref[h], F32))
        part = jnp.where(line == 0, high, jnp.where(line == 1, middle, jnp.where(line == 2, low, 0.0)))
        low_ref[STEP : STEP + 16, h * HEAD_DIM : (h + 1) * HEAD_DIM] = part.astype(BF16)
    l2 = []
    for fetch, held, at in ((fetch_k, k_ref, 0), (fetch_v, v_ref, COARSE)):
        fetch.wait()
        one = mm(half, held[...]).astype(BF16)
        low_ref[at : at + 64, :] = one
        two = mm(quarter, one).astype(BF16)
        low_ref[at + 64 : at + 96, :] = two
        l2.append(two)
    l3 = mm(quarter, jnp.concatenate(l2, axis=0)).astype(BF16)
    l3_ref[...] = l3
    l4 = mm(pooling(16, 32), l3).astype(BF16)
    l4_ref[...] = l4
    row, col = iota2(16, 16)
    l5 = mm(pooling(16, 16), l4).astype(BF16)
    m6 = mat((row < 8) & ((row & 3) < 2) & ((col >> 1) == ((row >> 2) * 2 + (row & 3))), 0.5)
    l6 = mm(m6, l5).astype(BF16)
    m7 = mat((row < 8) & ((row & 3) == 0) & ((col >> 1) == (row >> 1)), 0.5)
    l7 = mm(m7, l6).astype(BF16)
    b5, b6, b7 = l5[0:8], l6[0:8], l7[0:8]
    base7 = ((me >> 4) ^ 1) << 4
    base6 = ((me >> 3) ^ 1) << 3
    base5 = ((me >> 2) ^ 1) << 2
    base4 = (me >> 2) << 2
    for i in range(16):
        slot_ref[base7 + i] = b7
    for i in range(8):
        slot_ref[base6 + i] = b6
    for i in range(4):
        slot_ref[base5 + i] = b5
    for i in range(4):
        slot_ref[base4 + i] = jnp.zeros((8, WIDTH), BF16)


def far_column(me, line):
    at5 = ((((me >> 2) ^ 1) << 2) + (line >> 2)) * 8 + (line & 3)
    six = line - 16
    at6 = ((((me >> 3) ^ 1) << 3) + (six >> 1)) * 8 + (six & 1)
    at7 = ((((me >> 4) ^ 1) << 4) + (line - 32)) * 8
    return jnp.where(line < 16, at5, jnp.where(line < 32, at6, at7))


def local_kernel(q_hbm, c_hbm, k_hbm, v_hbm, low_ref, loc_ref, s_ref, v_ref, sems):
    moves = (
        (k_hbm, loc_ref.at[pl.ds(0, TOKENS)]),
        (q_hbm, loc_ref.at[pl.ds(QUERY, TOKENS)]),
        (v_hbm, v_ref.at[pl.ds(0, TOKENS)]),
        (c_hbm, loc_ref.at[pl.ds(COTANGENT, TOKENS)]),
    )
    fetches = [pltpu.make_async_copy(a, b, sems.at[i]) for i, (a, b) in enumerate(moves)]
    for fetch in fetches:
        fetch.start()
    loc_ref[TOKENS:LOCAL, :] = low_ref[0:COARSE, :]
    v_ref[TOKENS:LOCAL, :] = low_ref[COARSE : 2 * COARSE, :]
    loc_ref[STEPS : STEPS + 16, :] = low_ref[STEP : STEP + 16, :]
    lane = lax.broadcasted_iota(jnp.int32, (1, TOKENS), 1)
    quarter = lane >> 5
    lower = lane < 64


    def compact(full):
        def by_quarter(blocks):
            return jnp.where(
                quarter < 2,
                jnp.where(quarter == 0, blocks[0], blocks[1]),
                jnp.where(quarter == 2, blocks[2], blocks[3]),
            )

        zero = by_quarter([full[32 * g : 32 * g + 32] for g in range(4)])
        one = by_quarter([full[128 + 16 * (g ^ 1) : 144 + 16 * (g ^ 1)] for g in range(4)])
        two = jnp.where(lower, full[208:224], full[192:208])
        return zero, one, two

    step_all = jnp.sum(low_ref[STEP : STEP + 16, :].astype(F32), axis=0, keepdims=True)
    for which, (held, at) in enumerate(((loc_ref, QUERY), (v_ref, COTANGENT))):
        fetches[2 * which].wait()
        fetches[2 * which + 1].wait()
        for h in range(HEADS):
            sl = slice(h * HEAD_DIM, (h + 1) * HEAD_DIM)
            raw = mm(held[0:LOCAL, sl], loc_ref[at : at + TOKENS, sl], ((1,), (1,)))
            zero, one, two = compact(raw)
            if which == 0:
                step = step_all[:, sl]
                zero, one, two = zero * SCALE, one * SCALE + step, two * SCALE + 2 * step
            s_ref[64 * which : 64 * which + 64, sl] = jnp.concatenate([zero, one, two], axis=0)


def score_kernel(loc_ref, near_ref, r3_ref, r4a_ref, r4b_ref, r_ref, w_ref, s_ref):
    me = lax.axis_index("seq")
    row, col = iota2(FAR, PEERS * 8)
    place = far_column(me, row)
    far = r_ref[...]
    prow, pcol = iota2(16, 16)
    for which in range(2):
        at = REMOTE * which
        w_ref[at : at + 16, :] = r3_ref[16 * which : 16 * which + 16, :]
        first = mat((prow < 8) & (pcol == prow + 8 * which), 1.0)
        second = mat((prow >= 8) & (pcol == prow - 8 + 8 * which), 1.0)
        four = mm(first, r4a_ref[...]) + mm(second, r4b_ref[...])
        w_ref[at + 16 : at + 32, :] = four.astype(BF16)
        w_ref[at + 32 : at + 80, :] = mm(mat(col == place + 4 * which, 1.0), far).astype(BF16)
    step_all = jnp.sum(loc_ref[STEPS : STEPS + 16, :].astype(F32), axis=0, keepdims=True)
    total = [None] * HEADS
    for h in range(HEADS):
        sl = slice(h * HEAD_DIM, (h + 1) * HEAD_DIM)
        raw = mm(w_ref[0:REMOTE, sl], loc_ref[QUERY : QUERY + TOKENS, sl], ((1,), (1,)))
        step = step_all[:, sl]
        parts = [near_ref[0:64, sl]]
        parts += [raw[16 * i : 16 * i + 16] * SCALE + (i + 3) * step for i in range(5)]
        scores = jnp.concatenate(parts, axis=0)
        top = jnp.max(scores, axis=0, keepdims=True)
        expo = jnp.exp(scores - top)
        probs = expo * (1.0 / jnp.sum(expo, axis=0, keepdims=True))
        probs_b = probs.astype(BF16)
        raw = mm(w_ref[REMOTE : 2 * REMOTE, sl], loc_ref[COTANGENT : COTANGENT + TOKENS, sl], ((1,), (1,)))
        dprobs = jnp.concatenate([near_ref[64:128, sl], raw], axis=0)
        delta = jnp.sum(probs_b.astype(F32) * dprobs, axis=0, keepdims=True)
        dscores = probs * (dprobs - delta)
        w_ref[PROBS : PROBS + KEYS, sl] = probs_b
        w_ref[DSCORES : DSCORES + KEYS, sl] = dscores.astype(BF16)
        acc = None
        for level in range(1, LEVELS):
            at = 16 + 16 * level
            term = level * (dscores[at : at + 8] + dscores[at + 8 : at + 16])
            acc = term if acc is None else acc + term
        total[h] = jnp.sum(acc, axis=0, keepdims=True)
    tile = jnp.concatenate(total, axis=0)
    for i in range(s_ref.shape[0]):
        s_ref[i] = tile


def far_grad_kernel(loc_ref, w_ref, g3_ref, g4a_ref, g4b_ref, g5_ref, gf_ref):
    for h in range(HEADS):
        sl = slice(h * HEAD_DIM, (h + 1) * HEAD_DIM)
        q, c = loc_ref[QUERY : QUERY + TOKENS, sl], loc_ref[COTANGENT : COTANGENT + TOKENS, sl]
        dk = mm(w_ref[DSCORES + 64 : DSCORES + KEYS, sl], q) * SCALE
        dv = mm(w_ref[PROBS + 64 : PROBS + KEYS, sl], c)
        g3_ref[0:16, sl] = dk[0:16].astype(BF16)
        g3_ref[16:32, sl] = dv[0:16].astype(BF16)
        g4a_ref[:, sl] = jnp.concatenate([dk[16:24], dv[16:24]], axis=0).astype(BF16)
        g4b_ref[:, sl] = jnp.concatenate([dk[24:32], dv[24:32]], axis=0).astype(BF16)
        g5_ref[0:16, sl] = dk[32:48].astype(BF16)
        g5_ref[16:32, sl] = dv[32:48].astype(BF16)
        gf_ref[0:32, sl] = dk[48:80].astype(BF16)
        gf_ref[32:64, sl] = dv[48:80].astype(BF16)


def grad_kernel(loc_ref, w_ref, dq_ref, gk_ref, gv_ref):
    lane = lax.broadcasted_iota(jnp.int32, (1, TOKENS), 1)
    quarter = lane >> 5
    lower = lane < 64

    srow, scol = iota2(TOKENS, 96)
    spread = jnp.where(
        (scol < 64) & (scol == (srow >> 1)),
        0.5,
        jnp.where((scol >= 64) & (scol - 64 == (srow >> 2)), 0.25, 0.0),
    ).astype(BF16)

    def expand(part):
        part = part.astype(F32)
        zero, one, two = part[0:32], part[32:48], part[48:64]
        rows = [jnp.where(quarter == g, zero, 0.0) for g in range(4)]
        rows += [jnp.where(quarter == (g ^ 1), one, 0.0) for g in range(4)]
        rows += [jnp.where(lower, 0.0, two), jnp.where(lower, two, 0.0)]
        return jnp.concatenate(rows, axis=0).astype(BF16)

    for h in range(HEADS):
        sl = slice(h * HEAD_DIM, (h + 1) * HEAD_DIM)
        q, c = loc_ref[QUERY : QUERY + TOKENS, sl], loc_ref[COTANGENT : COTANGENT + TOKENS, sl]
        d_near = expand(w_ref[DSCORES : DSCORES + 64, sl])
        p_near = expand(w_ref[PROBS : PROBS + 64, sl])
        d_far = w_ref[DSCORES + 64 : DSCORES + KEYS, sl]
        dq = mm(d_near, loc_ref[0:LOCAL, sl], ((0,), (0,))) + mm(d_far, w_ref[0:REMOTE, sl], ((0,), (0,)))
        dq_ref[:, sl] = (dq * SCALE).astype(BF16)
        dk = mm(d_near, q) * SCALE
        dv = mm(p_near, c)
        gk_ref[:, sl] = dk[0:128] + mm(spread, dk[128:224].astype(BF16))
        gv_ref[:, sl] = dv[0:128] + mm(spread, dv[128:224].astype(BF16))


def slope_kernel(
    s_ref, gf_ref, r5_ref, g3_ref, g4a_ref, g4b_ref, pair_ref, a_ref, b_ref, slot_ref
):
    me = lax.axis_index("seq")
    row, col = iota2(PEERS * 8, 64)
    is_key = col < 32
    line = jnp.where(is_key, col, col - 32) + 16
    place = far_column(me, line) + jnp.where(is_key, 0, 2)
    first = mm(mat(row == place, 1.0), gf_ref[:, 0:HALF])
    second = mm(mat(row == place + 4, 1.0), gf_ref[:, HALF:WIDTH])
    slot_ref[:, 0:HALF] = (first + second).astype(BF16)
    value = jnp.sum(jnp.sum(s_ref[...], axis=0), axis=1, keepdims=True)
    high, middle, low = three_parts(value)
    lane = lax.broadcasted_iota(jnp.int32, (HEADS, 128), 1)
    tile = jnp.where(
        lane == 0, high, jnp.where(lane == 1, middle, jnp.where(lane == 2, low, 0.0))
    )
    slot_ref[:, HALF:] = jnp.concatenate([tile] * PEERS, axis=0).astype(BF16)
    row, col = iota2(16, 32)
    for apart, own_ref, out_ref in ((1, g3_ref, pair_ref), (2, g4a_ref, a_ref), (3, g4b_ref, b_ref)):
        size = own_ref.shape[0]
        out_ref[0:size, :] = own_ref[...]
        at = ((me & 3) ^ apart) * 4
        pick = ((row < 4) & (col == at + row)) | ((row >= 4) & (row < 8) & (col == at + row + 12))
        out_ref[size : size + 16, :] = mm(mat(pick, 1.0), r5_ref[...]).astype(BF16)


def final_kernel(
    gk_ref, gv_ref, pair_ref, a_ref, b_ref, r5_ref, r_ref, ok_ref, ov_ref, os_ref
):
    me = lax.axis_index("seq")
    row, col = iota2(TOKENS, PEERS * 8)
    apart = (col >> 3) ^ me
    line = col & 7
    shift = jnp.where(apart >= 16, 7, 6)
    weight = jnp.where(apart >= 16, 2.0**-7, jnp.where(apart >= 8, 2.0**-6, 0.0))
    covers = lax.shift_right_logical(row, shift)
    row3, col3 = iota2(TOKENS, 48)
    row4, col4 = iota2(TOKENS, 32)
    for out_ref, own_ref, which in ((ok_ref, gk_ref, 0), (ov_ref, gv_ref, 1)):
        near = own_ref[...]
        three = jnp.where((row3 >> 3) + 16 * which == col3, 2.0**-3, 0.0)
        five = jnp.where((row3 >> 5) + 32 + 4 * which == col3, 2.0**-5, 0.0)
        near += mm((three + five).astype(BF16), pair_ref[...])
        four = jnp.where((row4 >> 4) + 8 * which == col4, 2.0**-4, 0.0)
        five = jnp.where((row4 >> 5) + 16 + 4 * which == col4, 2.0**-5, 0.0)
        both = (four + five).astype(BF16)
        near += mm(both, a_ref[...]) + mm(both, b_ref[...])
        mine = mat((row4 >> 5) + 4 * (me & 3) + 16 * which == col4, 2.0**-5)
        near += mm(mine, r5_ref[...])
        for half in range(2):
            sl = slice(HALF * half, HALF * half + HALF)
            far = mat(covers + 2 * which + 4 * half == line, weight)
            out_ref[:, sl] = (near[:, sl] + mm(far, r_ref[:, 0:HALF])).astype(BF16)
    slopes = r_ref[:, HALF:].astype(F32).reshape(PEERS, HEADS, 128)
    value = jnp.sum(jnp.sum(slopes, axis=0), axis=1, keepdims=True)
    srow, scol = iota2(HEADS, 128)
    line = jnp.sum(jnp.where(srow == scol, value, 0.0), axis=0, keepdims=True)
    os_ref[...] = line[:, 0:HEADS]


def call(kernel, outs, ins, places=None, out_places=None, scratch=(), cost=1 << 20, alias=None, vmem=12):
    places = places or [pltpu.VMEM] * len(ins)
    out_places = out_places or [pltpu.VMEM] * len(outs)
    return pl.pallas_call(
        kernel,
        out_shape=[jax.ShapeDtypeStruct(s, t) for s, t in outs],
        in_specs=[pl.BlockSpec(memory_space=place) for place in places],
        out_specs=[pl.BlockSpec(memory_space=place) for place in out_places],
        scratch_shapes=list(scratch),
        input_output_aliases=alias or {},
        compiler_params=pltpu.CompilerParams(vmem_limit_bytes=vmem * 1024 * 1024),
        cost_estimate=pl.CostEstimate(flops=0, bytes_accessed=cost, transcendentals=0),
    )(*ins)


def swap(block, apart):
    return lax.ppermute(block, "seq", [(i, i ^ apart) for i in range(PEERS)])


def exchange(slots):
    width = slots.shape[-1]
    back = lax.all_to_all(slots.reshape(PEERS, 8, width), "seq", 0, 0)
    return back.reshape(PEERS * 8, width)


def per_device(queries, keys_in, values_in, cotangent, level_slope):
    q, k, v, c = queries[0], keys_in[0], values_in[0], cotangent[0]
    wide = WIDTH
    block = pltpu.VMEM((TOKENS, wide), BF16)
    low, l3, l4, slots = call(
        pool_kernel,
        [((STEP + 16, wide), BF16), ((32, wide), BF16), ((16, wide), BF16), ((PEERS, 8, wide), BF16)],
        (k, v, level_slope),
        [pl.ANY] * 3,
        scratch=[block, block, pltpu.SMEM((HEADS,), F32), pltpu.SemaphoreType.DMA((3,))],
        vmem=58,
    )
    far = exchange(slots)
    near3 = swap(l3, 1)
    near4a = swap(l4, 2)
    near4b = swap(l4, 3)
    loc, near = call(
        local_kernel,
        [((STEPS + 16, wide), BF16), ((128, wide), F32)],
        (q, c, k, v, low),
        [pl.ANY] * 4 + [pltpu.VMEM],
        scratch=[pltpu.VMEM((LOCAL, wide), BF16), pltpu.SemaphoreType.DMA((4,))],
        cost=LONG,
    )
    groups = lax.axis_size("dp")
    work, slopes = call(
        score_kernel,
        [((DSCORES + KEYS, wide), BF16), ((groups, HEADS, 128), F32)],
        (loc, near, near3, near4a, near4b, far),
    )
    slopes = lax.all_to_all(slopes, "dp", 0, 0)
    g3, g4a, g4b, g5, gf = call(
        far_grad_kernel,
        [((32, wide), BF16), ((16, wide), BF16), ((16, wide), BF16), ((32, wide), BF16), ((64, wide), BF16)],
        (loc, work),
    )
    near5 = swap(g5, 4)
    pair, four_a, four_b, slots = call(
        slope_kernel,
        [((48, wide), BF16), ((32, wide), BF16), ((32, wide), BF16), ((PEERS * 8, HALF + 128), BF16)],
        (slopes, gf, near5, g3, g4a, g4b),
    )
    far = exchange(slots)
    pair = swap(pair, 1)
    four_a = swap(four_a, 2)
    four_b = swap(four_b, 3)
    dq, gk, gv = call(
        grad_kernel,
        [((TOKENS, wide), BF16), ((TOKENS, wide), F32), ((TOKENS, wide), F32)],
        (loc, work),
        cost=LONG,
    )
    dk, dv, ds = call(
        final_kernel,
        [((TOKENS, wide), BF16), ((TOKENS, wide), BF16), ((1, HEADS), F32)],
        (gk, gv, pair, four_a, four_b, near5, far),
    )
    return dq[None], dk[None], dv[None], ds.reshape(HEADS)


def solution(mesh):
    row = P("dp", "seq", None)
    return jax.shard_map(
        per_device,
        mesh=mesh,
        in_specs=(row, row, row, row, P()),
        out_specs=(row, row, row, P()),
        check_vma=False,
    )
```
